32 devices in a mesh: aux: 4 (over z), bas: 8 (over y, x, core).
Axes of the slice: x: 2, y: 2, z: 4, core: 2. Of those that a mesh axis runs over, the one named last changes fastest.
Arguments:
- coefficients: bfloat16 [4096, 256], P('bas'), may hold values from -0.5 to 0.5
- tensor: bfloat16 [32, 32, 3, 128, 128], P('aux', 'bas'), may hold values from -0.62890625 to 0.62890625
- pattern: int32 [32, 3], replicated, may hold values from -1 to 31, as said below
Outputs:
- exchange_tiles: float32 [32, 3, 128, 128], P('bas')
The draws below stay inside these ranges and needn't reach their ends.
Inputs may be any that keep to these rules, and one draw needn't show every extreme that they name: `pattern`: row m lists distinct basis blocks that lie in [(4 * (m // 4) - 4), (4 * (m // 4) + 8)); its filled slots come first and its empty slots (-1) last. Rows hold from 1 to 3 filled slots; some row is full.
All inputs are finite; a program needn't handle non-finite values.
Results may differ from the reference program's by a relative error of at most 0.0012.
Values may be sent and summed in bfloat16 or wider, within the bound.
No kernel may reach another device: no remote copies, remote signals or barrier semaphores. Data moves between devices by JAX's collectives and lax.ppermute only.
A program may use at most 64 MiB of HBM per device.

```python
import jax
import jax.numpy as jnp
from jax import lax

OCC = 256
BLK = 128
MB = 4
NP = 3
PA = 8
NBB = 32
NBAS = 4096
NAUX = 32
N_AUX = 4
N_BAS = 8


def draw_pattern(key, part):
    key = jax.random.fold_in(key, 11)
    key_pick, key_live = jax.random.split(key)
    block_count = MB * N_BAS
    block_index = jnp.arange(block_count, dtype=jnp.int32)
    owner_block = block_index // MB
    spread_index = jnp.arange(3 * MB, dtype=jnp.int32)
    candidate = (owner_block[:, None] - 1) * MB + spread_index[None, :]
    in_range = (candidate >= 0) & (candidate < block_count)
    scores = jax.random.randint(key_pick, (block_count, 3 * MB), 0, 2 ** 20) * (4 * MB) + spread_index[None, :]
    scores = jnp.where(in_range, scores, -1 - spread_index[None, :])
    scores = scores.at[block_count - 1, 2 * MB - 1].set(2 ** 30)
    top_values, top_index = lax.top_k(scores, NP)
    chosen = jnp.take_along_axis(candidate, top_index, axis=1)
    live_count = jax.random.randint(key_live, (block_count,), 1, NP + 1)
    live_count = live_count.at[0].set(NP).at[block_count - 1].set(NP).at[1].set(1)
    slot_index = jnp.arange(NP, dtype=jnp.int32)
    return jnp.where(slot_index[None, :] < live_count[:, None], chosen, -1).astype(jnp.int32)


def steps_of(stream_key, dims, pieces, low, high):
    level, own = 1.0, jax.random.fold_in(stream_key, 6)
    for position, shards_of in pieces:
        heights = jnp.exp(jax.random.uniform(jax.random.fold_in(own, position), (shards_of,), jnp.float32, low / len(pieces), high / len(pieces)))
        level = level * jnp.repeat(heights, dims[position] // shards_of).reshape([-1 if axis == position else 1 for axis in range(len(dims))])
    return level


def scatter_about(own_key, shape, spread, most, shards=(), kind=jnp.bfloat16):
    array = jax.random.normal(own_key, shape, jnp.float32) * spread
    if len(shards) > 0:
        array = steps_of(own_key, shape, shards, -0.22, 0.18) * array
    return jnp.clip(array, min=-most, max=most).astype(kind)


def setup_inputs(seed: int = 0) -> dict:
    streams_of = jax.random.split(jax.random.key(seed), 4)
    coefficients = scatter_about(streams_of[0], (NBAS, OCC), BLK ** -0.5, 0.5, ((0, 8),))
    tensor = scatter_about(streams_of[1], (NAUX, NBB, NP, BLK, BLK), ((PA * N_AUX * OCC) ** -0.25), 0.62890625, ((0, 4), (1, 8)))
    pattern = draw_pattern(jax.random.fold_in(streams_of[3], 71), 0)
    return {"coefficients": coefficients, "tensor": tensor, "pattern": pattern}


def reference(coefficients, tensor, pattern):
    block_count = pattern.shape[0]
    coeff_blocks = coefficients.reshape(block_count, BLK, OCC)
    safe_index = jnp.maximum(pattern, 0)
    live_slot = (pattern >= 0).astype(jnp.float32)

    def half_block(row):
        selected = coeff_blocks[safe_index[row]].astype(jnp.float32) * live_slot[row][:, None, None]
        aux_part = lax.dynamic_index_in_dim(tensor, row, 1, keepdims=False).astype(jnp.float32)
        return jnp.einsum("pjab,jbi->pai", aux_part, selected).astype(jnp.bfloat16)

    half_form = lax.map(half_block, jnp.arange(block_count, dtype=jnp.int32))

    def tile_block(row):
        owned_half = half_form[row].astype(jnp.float32)
        partner = half_form[safe_index[row]].astype(jnp.float32) * live_slot[row][:, None, None, None]
        return jnp.einsum("pai,jpci->jac", owned_half, partner)

    return lax.map(tile_block, jnp.arange(block_count, dtype=jnp.int32))
```

```python
import functools

import jax
import jax.numpy as jnp
from jax import lax
from jax.experimental import pallas as pl
from jax.experimental.pallas import tpu as pltpu
from jax.sharding import PartitionSpec as P

CHUNKS = 2
SCALE_ROWS = 16
VMEM = pl.BlockSpec(memory_space=pltpu.VMEM)
SMEM = pl.BlockSpec(memory_space=pltpu.SMEM)


def params(mib):
    return pltpu.CompilerParams(vmem_limit_bytes=mib << 20)


def half_kernel(pattern, own, beside, across, tensor, whole, *rest):
    parts, chosen = rest[:-1], rest[-1]
    aux, blocks, slots, width, _ = tensor.shape
    occupied = own.shape[1]
    rows, columns = parts[0].shape[1:]
    device = lax.axis_index("bas")
    for m in range(blocks):
        for j in range(slots):
            place = pattern[device * blocks + m, j]
            group, start = place // blocks, pl.multiple_of((place % blocks) * width, width)
            into = chosen.at[pl.ds(j * width, width)]

            @pl.when(place < 0)
            def _():
                into[...] = jnp.zeros((width, occupied), jnp.bfloat16)

            for source, held in (
                (own, group == device),
                (beside, group == device ^ 1),
                (across, (group != device) & (group != device ^ 1)),
            ):

                @pl.when((place >= 0) & held)
                def _():
                    into[...] = source[pl.ds(start, width), :]

        for p in range(aux):
            row = jnp.concatenate([tensor[p, m, j] for j in range(slots)], axis=1)
            half = jnp.dot(row, chosen[...], preferred_element_type=jnp.float32)
            half = half.astype(jnp.bfloat16)
            whole[m, :, p * occupied : (p + 1) * occupied] = half
            unit, column = divmod(p * occupied, columns)
            for k in range(width // rows):
                parts[2 * k + unit][m, :, column : column + occupied] = half[k * rows : (k + 1) * rows]


def half_forms(pattern, own, beside, across, tensor):
    aux, blocks, slots, width, _ = tensor.shape
    occupied = own.shape[1]
    part = jax.ShapeDtypeStruct((blocks, width // CHUNKS, aux * occupied // 2), jnp.bfloat16)
    out = [jax.ShapeDtypeStruct((blocks, width, aux * occupied), jnp.bfloat16)] + [part] * (2 * CHUNKS)
    return pl.pallas_call(
        half_kernel,
        out_shape=out,
        in_specs=[SMEM] + [VMEM] * 4,
        out_specs=[VMEM] * len(out),
        scratch_shapes=[pltpu.VMEM((slots * width, occupied), jnp.bfloat16)],
        compiler_params=params(24),
    )(pattern, own, beside, across, tensor)


def encode(tiles, coded, scales):
    rows = tiles[0].shape[0]
    scales[...] = jnp.zeros_like(scales)
    for t, tile in enumerate(tiles):
        most = jnp.max(jnp.abs(tile), axis=0, keepdims=True)
        power = jnp.ceil(jnp.log2(jnp.maximum(most, 2.0**-90)))
        scales[t : t + 1, :] = power
        whole = jnp.round(tile * jnp.exp2(14.0 - power))
        coded[t * rows : (t + 1) * rows, :] = whole.astype(jnp.int32).astype(jnp.int16)
    end = len(tiles) * rows
    coded[end : end + SCALE_ROWS, :] = scales[...].astype(jnp.int32).astype(jnp.int16)


def decode(coded, rows, count):
    end = count * rows
    scales = coded[end : end + SCALE_ROWS, :].astype(jnp.int32).astype(jnp.float32)
    scales = jnp.exp2(scales - 14.0)
    for t in range(count):
        value = coded[t * rows : (t + 1) * rows, :].astype(jnp.int32).astype(jnp.float32)
        yield value * scales[t : t + 1, :]


def tile_kernel(relays, chunk, pattern, whole, beside, first, second, third, kept, sent, partner, scales):
    blocks, width, depth = whole.shape
    rows = first.shape[1]
    slots = partner.shape[0] // rows
    device, layer = lax.axis_index("bas"), lax.axis_index("aux")
    at = chunk * rows
    relayed = device < 0
    for target in relays:
        relayed = relayed | (device == target)
    tiles = []
    for m in range(blocks):
        for j in range(slots):
            place = pattern[device * blocks + m, j]
            group, block = place // blocks, jnp.maximum(place, 0) % blocks
            into = partner.at[pl.ds(j * rows, rows)]
            across = (place >= 0) & (group != device) & (group != device ^ 1)

            @pl.when(place < 0)
            def _():
                into[...] = jnp.zeros((rows, depth), jnp.bfloat16)

            @pl.when((place >= 0) & (group == device))
            def _():
                into[...] = whole[block, at : at + rows, :]

            @pl.when((place >= 0) & (group == device ^ 1))
            def _():
                into[...] = beside[block, at : at + rows, :]

            @pl.when(across)
            def _():
                into[:, : depth // 2] = first[block]

            if relays:

                @pl.when(across & relayed)
                def _():
                    into[:, depth // 2 :] = third[block]

            @pl.when(across & jnp.logical_not(relayed))
            def _():
                into[:, depth // 2 :] = second[block]

        product = lax.dot_general(
            partner[...], whole[m], (((1,), (1,)), ((), ())), preferred_element_type=jnp.float32
        )
        tiles += [product[j * rows : (j + 1) * rows] for j in range(slots)]
    half = len(tiles) // 2
    for parity in range(2):

        @pl.when(layer % 2 == parity)
        def _():
            mine, other = tiles[parity * half :][:half], tiles[(1 - parity) * half :][:half]
            for t in range(half):
                kept[t * rows : (t + 1) * rows, :] = mine[t]
            encode(other, sent, scales)


def chunk_tiles(relays, chunk, pattern, whole, beside, first, second, third):
    blocks, width, depth = whole.shape
    rows, slots = first.shape[1], pattern.shape[1]
    half = blocks * slots // 2
    return pl.pallas_call(
        functools.partial(tile_kernel, relays, chunk),
        out_shape=[
            jax.ShapeDtypeStruct((half * rows, width), jnp.float32),
            jax.ShapeDtypeStruct((half * rows + SCALE_ROWS, width), jnp.int16),
        ],
        in_specs=[SMEM] + [VMEM] * 5,
        out_specs=[VMEM] * 2,
        scratch_shapes=[
            pltpu.VMEM((slots * rows, depth), jnp.bfloat16),
            pltpu.VMEM((SCALE_ROWS, width), jnp.float32),
        ],
        compiler_params=params(24),
    )(pattern, whole, beside, first, second, third)


def add_kernel(count, mine, other, coded, scales):
    rows = (coded.shape[0] - SCALE_ROWS) // count
    if mine.dtype == jnp.float32:
        held = [mine[t * rows : (t + 1) * rows, :] for t in range(count)]
    else:
        held = decode(mine, rows, count)
    encode([a + b for a, b in zip(held, decode(other, rows, count))], coded, scales)


def add_coded(count, mine, other):
    return pl.pallas_call(
        functools.partial(add_kernel, count),
        out_shape=jax.ShapeDtypeStruct(other.shape, other.dtype),
        in_specs=[VMEM] * 2,
        out_specs=VMEM,
        scratch_shapes=[pltpu.VMEM((SCALE_ROWS, other.shape[1]), jnp.float32)],
        compiler_params=params(8),
    )(mine, other)


def final_kernel(*refs):
    coded, out, turned = refs[:-2], refs[-2], refs[-1]
    blocks, slots, width, _ = out.shape
    half = blocks * slots // 2
    chunks = len(coded) // 2
    rows = width // chunks
    layer = lax.axis_index("aux")
    for parity in range(2):

        @pl.when(layer % 2 == parity)
        def _():
            for mine in range(2):
                base = (parity if mine == 0 else 1 - parity) * half
                for k in range(chunks):
                    for t, tile in enumerate(decode(coded[2 * k + mine], rows, half)):
                        turned[base + t, k * rows : (k + 1) * rows, :] = tile

    for t in range(2 * half):
        out[t // slots, t % slots] = turned[t].T


def final_tiles(shape, coded):
    blocks, slots, width, _ = shape
    return pl.pallas_call(
        final_kernel,
        out_shape=jax.ShapeDtypeStruct(shape, jnp.float32),
        in_specs=[VMEM] * len(coded),
        out_specs=VMEM,
        scratch_shapes=[pltpu.VMEM((blocks * slots, width, width), jnp.float32)],
        compiler_params=params(8),
    )(*coded)


def flipped(size, mask):
    return [(i, i ^ mask) for i in range(size)]


def body(coefficients, tensor, pattern):
    devices, layers = lax.axis_size("bas"), lax.axis_size("aux")
    _, blocks, slots, width, _ = tensor.shape
    chip = flipped(devices, 1)
    across = [pair for i in range(1, devices - 1, 2) for pair in ((i, i + 1), (i + 1, i))]
    detours = ((3, 4, 7), (4, 3, 0)) if devices == 8 else ()
    second_way = [pair for pair in across if pair not in [d[:2] for d in detours]]
    second_way += [(source, via) for source, _, via in detours]
    last_way = [(via, target) for _, target, via in detours]
    relays = tuple(target for _, target, _ in detours)

    beside = lax.ppermute(coefficients, "bas", chip)
    beyond = lax.ppermute(coefficients, "bas", across)
    whole, *parts = half_forms(pattern, coefficients, beside, beyond, tensor)
    arrived = []
    for k in range(CHUNKS):
        second = lax.ppermute(parts[2 * k + 1], "bas", second_way)
        first = lax.ppermute(parts[2 * k], "bas", across)
        third = lax.ppermute(second, "bas", last_way) if detours else second
        arrived.append((first, second, third))
    partner = lax.ppermute(whole, "bas", chip)
    half = blocks * slots // 2
    coded = []
    for k in range(CHUNKS):
        kept, sent = chunk_tiles(relays, k, pattern, whole, partner, *arrived[k])
        mine = add_coded(half, kept, lax.ppermute(sent, "aux", flipped(layers, 1)))
        mask = 2
        while mask < layers:
            mine = add_coded(half, mine, lax.ppermute(mine, "aux", flipped(layers, mask)))
            mask *= 2
        coded += [mine, lax.ppermute(mine, "aux", flipped(layers, 1))]
    return final_tiles((blocks, slots, width, width), coded)


def solution(mesh):
    return jax.shard_map(
        body,
        mesh=mesh,
        in_specs=(P("bas", None), P("aux", "bas", None, None, None), P()),
        out_specs=P("bas", None, None, None),
        check_vma=False,
    )
```

```python
import functools

import jax
import jax.numpy as jnp
from jax import lax
from jax.experimental import pallas as pl
from jax.experimental.pallas import tpu as pltpu
from jax.sharding import PartitionSpec as P

CUTS = (0, 64, 128)
SCALE_ROWS = 16
FULL = 32752.0
VMEM = pl.BlockSpec(memory_space=pltpu.VMEM)
ANY = pl.BlockSpec(memory_space=pl.ANY)
SMEM = pl.BlockSpec(memory_space=pltpu.SMEM)


def params(mib):
    return pltpu.CompilerParams(vmem_limit_bytes=mib << 20)


def fetch_kernel(tensor, own, tensor_out, own_out, sems):
    copies = [
        pltpu.make_async_copy(own, own_out, sems.at[0]),
        pltpu.make_async_copy(tensor, tensor_out, sems.at[1]),
    ]
    for copy in copies:
        copy.start()
    for copy in copies:
        copy.wait()


def fetch(tensor, own):
    arrays = (tensor, own)
    return pl.pallas_call(
        fetch_kernel,
        out_shape=[jax.ShapeDtypeStruct(a.shape, a.dtype) for a in arrays],
        in_specs=[ANY] * 2,
        out_specs=[VMEM] * 2,
        scratch_shapes=[pltpu.SemaphoreType.DMA((2,))],
        compiler_params=params(8),
    )(*arrays)


def half_kernel(start, rows, earlier, pattern, own, beside, across, tensor, *rest):
    before, (out_0, out_1, *joined, chosen) = rest[:earlier], rest[earlier:]
    aux, blocks, slots, width, _ = tensor.shape
    occupied = own.shape[1]
    device = lax.axis_index("bas")
    for m in range(blocks):
        for j in range(slots):
            place = pattern[device * blocks + m, j]
            group, first = place // blocks, pl.multiple_of((place % blocks) * width, width)
            into = chosen.at[m, pl.ds(j * width, width)]

            @pl.when(place < 0)
            def _():
                into[...] = jnp.zeros((width, occupied), jnp.bfloat16)

            for source, held in (
                (own, group == device),
                (beside, group == device ^ 1),
                (across, (group != device) & (group != device ^ 1)),
            ):

                @pl.when((place >= 0) & held)
                def _():
                    into[...] = source[pl.ds(first, width), :]

        row = jnp.concatenate(
            [tensor[:, m, j, start : start + rows].reshape(aux * rows, width) for j in range(slots)], axis=1
        )
        half = jnp.dot(row, chosen[m], preferred_element_type=jnp.float32).astype(jnp.bfloat16)
        for p in range(aux):
            out, column = (out_0, p) if p < aux // 2 else (out_1, p - aux // 2)
            piece = half[p * rows : (p + 1) * rows]
            out[m, :, column * occupied : (column + 1) * occupied] = piece
            for whole in joined:
                whole[m, start : start + rows, p * occupied : (p + 1) * occupied] = piece
    for whole in joined:
        depth = aux * occupied // 2
        at = 0
        for one, other in zip(before[::2], before[1::2]):
            whole[:, at : at + one.shape[1], :depth] = one[...]
            whole[:, at : at + one.shape[1], depth:] = other[...]
            at += one.shape[1]


def half_forms(start, rows, pattern, own, beside, across, tensor, before=()):
    aux, blocks, slots, width, _ = tensor.shape
    occupied = own.shape[1]
    out = [jax.ShapeDtypeStruct((blocks, rows, aux * occupied // 2), jnp.bfloat16)] * 2
    if start + rows == width:
        out += [jax.ShapeDtypeStruct((blocks, width, aux * occupied), jnp.bfloat16)]
    return pl.pallas_call(
        functools.partial(half_kernel, start, rows, len(before)),
        out_shape=out,
        in_specs=[SMEM] + [VMEM] * (4 + len(before)),
        out_specs=[VMEM] * len(out),
        scratch_shapes=[pltpu.VMEM((blocks, slots * width, occupied), jnp.bfloat16)],
        compiler_params=params(24),
    )(pattern, own, beside, across, tensor, *before)


def encode(tiles, coded, scales):
    rows = tiles[0].shape[0]
    scales[...] = jnp.zeros_like(scales)
    for t, tile in enumerate(tiles):
        most = jnp.max(jnp.abs(tile), axis=0, keepdims=True)
        power = jnp.ceil(jnp.log2(jnp.maximum(most, 2.0**-90)))
        scales[t : t + 1, :] = power
        whole = jnp.round(tile * (FULL * jnp.exp2(-power)))
        coded[t * rows : (t + 1) * rows, :] = whole.astype(jnp.int32).astype(jnp.int16)
    end = len(tiles) * rows
    coded[end : end + SCALE_ROWS, :] = scales[...].astype(jnp.int32).astype(jnp.int16)


def decode(coded, rows, count):
    end = count * rows
    scales = coded[end : end + SCALE_ROWS, :].astype(jnp.int32).astype(jnp.float32)
    scales = jnp.exp2(scales) * (1.0 / FULL)
    for t in range(count):
        value = coded[t * rows : (t + 1) * rows, :].astype(jnp.int32).astype(jnp.float32)
        yield value * scales[t : t + 1, :]


def times(rows, whole):
    blocks, width, depth = whole.shape
    return lax.dot_general(
        rows, whole.reshape(blocks * width, depth), (((1,), (1,)), ((), ())), preferred_element_type=jnp.float32
    )


def near_kernel(cuts, whole, beside, *products):
    blocks, width, depth = whole.shape
    for k, product in enumerate(products):
        rows = cuts[k + 1] - cuts[k]
        for i, source in enumerate((whole, beside)):
            part = source[:, cuts[k] : cuts[k + 1], :].reshape(blocks * rows, depth)
            product[i * blocks * rows : (i + 1) * blocks * rows, :] = times(part, whole[...])


def near_products(cuts, whole, beside):
    blocks, width, _ = whole.shape
    return pl.pallas_call(
        functools.partial(near_kernel, cuts),
        out_shape=[
            jax.ShapeDtypeStruct((2 * blocks * (b - a), blocks * width), jnp.float32)
            for a, b in zip(cuts, cuts[1:])
        ],
        in_specs=[VMEM] * 2,
        out_specs=[VMEM] * (len(cuts) - 1),
        compiler_params=params(24),
    )(whole, beside)


def tile_kernel(relays, pattern, whole, near, first, second, third, kept, sent, far, scales):
    blocks, width, depth = whole.shape
    _, rows, cut = first.shape
    slots = pattern.shape[1]
    device, layer = lax.axis_index("bas"), lax.axis_index("aux")
    half = blocks * slots // 2
    far[...] = times(first[...].reshape(blocks * rows, cut), whole[:, :, :cut])

    def add(source):
        far[...] += times(source[...].reshape(blocks * rows, cut), whole[:, :, cut:])

    if relays:
        relayed = functools.reduce(jnp.logical_or, [device == target for target in relays])
        pl.when(relayed)(lambda: add(third))
        pl.when(jnp.logical_not(relayed))(lambda: add(second))
    else:
        add(second)

    def tile(t, parity):
        m = parity * (blocks // 2) + t // slots
        place = pattern[device * blocks + m, t % slots]
        group, block = place // blocks, jnp.maximum(place, 0) % blocks
        columns = pl.ds(pl.multiple_of(m * width, width), width)
        close = block + jnp.where(group == device, 0, blocks)
        inside = near[pl.ds(pl.multiple_of(close * rows, rows), rows), columns]
        outside = far[pl.ds(pl.multiple_of(block * rows, rows), rows), columns]
        value = jnp.where((group == device) | (group == device ^ 1), inside, outside)
        return jnp.where(place < 0, 0.0, value)

    for t in range(half):
        kept[t * rows : (t + 1) * rows, :] = tile(t, layer % 2)
    encode([tile(t, 1 - layer % 2) for t in range(half)], sent, scales)


def chunk_tiles(relays, pattern, whole, near, first, second, third):
    blocks, width, _ = whole.shape
    rows, slots = first.shape[1], pattern.shape[1]
    half = blocks * slots // 2
    return pl.pallas_call(
        functools.partial(tile_kernel, relays),
        out_shape=[
            jax.ShapeDtypeStruct((half * rows, width), jnp.float32),
            jax.ShapeDtypeStruct((half * rows + SCALE_ROWS, width), jnp.int16),
        ],
        in_specs=[SMEM] + [VMEM] * 5,
        out_specs=[VMEM] * 2,
        scratch_shapes=[
            pltpu.VMEM((blocks * rows, blocks * width), jnp.float32),
            pltpu.VMEM((SCALE_ROWS, width), jnp.float32),
        ],
        compiler_params=params(24),
    )(pattern, whole, near, first, second, third)


def add_kernel(count, mine, other, coded, scales):
    rows = (coded.shape[0] - SCALE_ROWS) // count
    if mine.dtype == jnp.float32:
        held = [mine[t * rows : (t + 1) * rows, :] for t in range(count)]
    else:
        held = decode(mine, rows, count)
    encode([a + b for a, b in zip(held, decode(other, rows, count))], coded, scales)


def add_coded(count, mine, other):
    return pl.pallas_call(
        functools.partial(add_kernel, count),
        out_shape=jax.ShapeDtypeStruct(other.shape, other.dtype),
        in_specs=[VMEM] * 2,
        out_specs=VMEM,
        scratch_shapes=[pltpu.VMEM((SCALE_ROWS, other.shape[1]), jnp.float32)],
        compiler_params=params(8),
    )(mine, other)


def final_kernel(*refs):
    coded, out, turned = refs[:-2], refs[-2], refs[-1]
    blocks, slots, width, _ = out.shape
    half = blocks * slots // 2
    layer = lax.axis_index("aux")
    for parity in range(2):

        @pl.when(layer % 2 == parity)
        def _():
            for mine in range(2):
                base = (parity if mine == 0 else 1 - parity) * half
                at = 0
                for part in coded[mine::2]:
                    rows = (part.shape[0] - SCALE_ROWS) // half
                    for t, tile in enumerate(decode(part, rows, half)):
                        turned[base + t, at : at + rows, :] = tile
                    at += rows

    for t in range(2 * half):
        out[t // slots, t % slots] = turned[t].T


def final_tiles(shape, coded):
    blocks, slots, width, _ = shape
    return pl.pallas_call(
        final_kernel,
        out_shape=jax.ShapeDtypeStruct(shape, jnp.float32),
        in_specs=[VMEM] * len(coded),
        out_specs=VMEM,
        scratch_shapes=[pltpu.VMEM((blocks * slots, width, width), jnp.float32)],
        compiler_params=params(8),
    )(*coded)


def flipped(size, mask):
    return [(i, i ^ mask) for i in range(size)]


def body(coefficients, tensor, pattern):
    devices, layers = lax.axis_size("bas"), lax.axis_size("aux")
    _, blocks, slots, width, _ = tensor.shape
    chip = flipped(devices, 1)
    across = [pair for i in range(1, devices - 1, 2) for pair in ((i, i + 1), (i + 1, i))]
    detours = ((3, 4, 7), (4, 3, 0)) if devices == 8 else ()
    second_way = [pair for pair in across if pair not in [d[:2] for d in detours]]
    second_way += [(source, via) for source, _, via in detours]
    last_way = [(via, target) for _, target, via in detours]
    relays = tuple(target for _, target, _ in detours)

    beyond = lax.ppermute(coefficients, "bas", across)
    beside = lax.ppermute(coefficients, "bas", chip)
    tensor, coefficients = fetch(tensor, coefficients)
    operands = (pattern, coefficients, beside, beyond, tensor)
    cuts = CUTS
    parts, arrived = [], []
    for a, b in zip(cuts, cuts[1:]):
        one, other, *joined = half_forms(a, b - a, *operands, before=parts if b == width else ())
        parts += [one, other]
        second = lax.ppermute(other, "bas", second_way)
        first = lax.ppermute(one, "bas", across)
        third = lax.ppermute(second, "bas", last_way) if detours else second
        arrived.append((first, second, third))
    (whole,) = joined
    near = near_products(cuts, whole, lax.ppermute(whole, "bas", chip))
    half = blocks * slots // 2
    coded = []
    for close, held in zip(near, arrived):
        kept, sent = chunk_tiles(relays, pattern, whole, close, *held)
        mine = add_coded(half, kept, lax.ppermute(sent, "aux", flipped(layers, 1)))
        mask = 2
        while mask < layers:
            mine = add_coded(half, mine, lax.ppermute(mine, "aux", flipped(layers, mask)))
            mask *= 2
        coded += [mine, lax.ppermute(mine, "aux", flipped(layers, 1))]
    return final_tiles((blocks, slots, width, width), coded)


def solution(mesh):
    return jax.shard_map(
        body,
        mesh=mesh,
        in_specs=(P("bas", None), P("aux", "bas", None, None, None), P()),
        out_specs=P("bas", None, None, None),
        check_vma=False,
    )
```

```python
import functools

import jax
import jax.numpy as jnp
from jax import lax
from jax.experimental import pallas as pl
from jax.experimental.pallas import tpu as pltpu
from jax.sharding import PartitionSpec as P

CUT = 64
PIECES = 2
SCALE_ROWS = 16
FULL = 32752.0
VMEM = pl.BlockSpec(memory_space=pltpu.VMEM)
ANY = pl.BlockSpec(memory_space=pl.ANY)
SMEM = pl.BlockSpec(memory_space=pltpu.SMEM)


def params(mib):
    return pltpu.CompilerParams(vmem_limit_bytes=mib << 20)


NO_COST = pl.CostEstimate(flops=0, bytes_accessed=0, transcendentals=0)


def fetch_kernel(tensor, own, tensor_out, own_out, sems):
    copies = [
        pltpu.make_async_copy(own, own_out, sems.at[0]),
        pltpu.make_async_copy(tensor, tensor_out, sems.at[1]),
    ]
    for copy in copies:
        copy.start()
    for copy in copies:
        copy.wait()


def fetch(tensor, own):
    arrays = (tensor, own)
    return pl.pallas_call(
        fetch_kernel,
        out_shape=[jax.ShapeDtypeStruct(a.shape, a.dtype) for a in arrays],
        in_specs=[ANY] * 2,
        out_specs=[VMEM] * 2,
        scratch_shapes=[pltpu.SemaphoreType.DMA((2,))],
        compiler_params=params(8),
        cost_estimate=NO_COST,
    )(*arrays)


def half_kernel(cuts, pattern, own, beside, across, tensor, *outs):
    parts, pieces = outs[: len(cuts) - 1], outs[len(cuts) - 1 :]
    aux, blocks, slots, width, _ = tensor.shape
    occupied = own.shape[1]
    device = lax.axis_index("bas")
    for m in range(blocks):
        chosen = []
        for j in range(slots):
            place = pattern[(device * blocks + m) * slots + j]
            group = place // blocks
            rows = pl.ds(pl.multiple_of(jnp.maximum(place, 0) % blocks * width, width), width)
            value = jnp.where(group == device ^ 1, beside[rows, :], across[rows, :])
            value = jnp.where(group == device, own[rows, :], value)
            chosen.append(jnp.where(place < 0, jnp.zeros_like(value), value))
        chosen = jnp.concatenate(chosen, axis=0)
        for p in range(aux):
            row = jnp.concatenate([tensor[p, m, j] for j in range(slots)], axis=1)
            half = jnp.dot(row, chosen, preferred_element_type=jnp.float32).astype(jnp.bfloat16)
            piece, column = divmod(p, aux // len(pieces))
            pieces[piece][m, :, column * occupied : (column + 1) * occupied] = half
            for part, start, stop in zip(parts, cuts, cuts[1:]):
                part[m, :, p * occupied : (p + 1) * occupied] = half[start:stop]


def half_forms(cuts, pattern, own, beside, across, tensor):
    aux, blocks, slots, width, _ = tensor.shape
    depth = aux * own.shape[1]
    shapes = [(blocks, b - a, depth) for a, b in zip(cuts, cuts[1:])]
    shapes += [(blocks, width, depth // PIECES)] * PIECES
    outs = pl.pallas_call(
        functools.partial(half_kernel, cuts),
        out_shape=[jax.ShapeDtypeStruct(shape, jnp.bfloat16) for shape in shapes],
        in_specs=[SMEM] + [VMEM] * 4,
        out_specs=[VMEM] * len(shapes),
        compiler_params=params(24),
        cost_estimate=NO_COST,
    )(pattern, own, beside, across, tensor)
    return outs[:-PIECES], outs[-PIECES:]


def encode(tiles, coded, scales):
    rows = tiles[0].shape[0]
    scales[...] = jnp.zeros_like(scales)
    for t, tile in enumerate(tiles):
        most = jnp.max(jnp.abs(tile), axis=0, keepdims=True)
        power = jnp.ceil(jnp.log2(jnp.maximum(most, 2.0**-90)))
        scales[t : t + 1, :] = power
        whole = jnp.round(tile * (FULL * jnp.exp2(-power)))
        coded[t * rows : (t + 1) * rows, :] = whole.astype(jnp.int32).astype(jnp.int16)
    end = len(tiles) * rows
    coded[end : end + SCALE_ROWS, :] = scales[...].astype(jnp.int32).astype(jnp.int16)


def decode(coded, rows, count):
    end = count * rows
    scales = coded[end : end + SCALE_ROWS, :].astype(jnp.int32).astype(jnp.float32)
    scales = jnp.exp2(scales) * (1.0 / FULL)
    for t in range(count):
        value = coded[t * rows : (t + 1) * rows, :].astype(jnp.int32).astype(jnp.float32)
        yield value * scales[t : t + 1, :]


def times(rows, pieces):
    total = 0.0
    for k, piece in enumerate(pieces):
        left, right = rows(k), piece[...]
        total += lax.dot_general(
            left.reshape(-1, left.shape[2]),
            right.reshape(-1, right.shape[2]),
            (((1,), (1,)), ((), ())),
            preferred_element_type=jnp.float32,
        )
    return total


def near_kernel(start, stop, *refs):
    whole, beside, product = refs[:PIECES], refs[PIECES : 2 * PIECES], refs[-1]
    half = product.shape[0] // 2
    product[:half, :] = times(lambda k: whole[k][:, start:stop, :], whole)
    product[half:, :] = times(lambda k: beside[k][:, start:stop, :], whole)


def near_products(start, stop, whole, beside, *earlier):
    blocks, width, _ = whole[0].shape
    return pl.pallas_call(
        functools.partial(near_kernel, start, stop),
        out_shape=jax.ShapeDtypeStruct((2 * blocks * (stop - start), blocks * width), jnp.float32),
        in_specs=[VMEM] * (2 * PIECES) + [ANY] * len(earlier),
        out_specs=VMEM,
        compiler_params=params(24),
        cost_estimate=NO_COST,
    )(*whole, *beside, *earlier)


def gate_kernel(_, out):
    out[...] = jnp.zeros_like(out)


def gate(earlier):
    return pl.pallas_call(
        gate_kernel,
        out_shape=jax.ShapeDtypeStruct((8, 128), jnp.float32),
        in_specs=[ANY],
        out_specs=VMEM,
        compiler_params=params(4),
        cost_estimate=NO_COST,
    )(earlier)


def tile_kernel(relays, count, pattern, near, *refs):
    whole, across, (kept, sent, far, scales, places, sem) = refs[:PIECES], refs[PIECES : PIECES + count], refs[-6:]
    blocks, width, depth = whole[0].shape
    rows = across[0].shape[1]
    slots = pattern.shape[0] // (blocks * lax.axis_size("bas"))
    device, layer = lax.axis_index("bas"), lax.axis_index("aux")
    half = blocks * slots // 2
    copy = pltpu.make_async_copy(pattern, places, sem)
    copy.start()

    def multiply(source):
        far[...] = times(lambda k: source[:, :, k * depth : (k + 1) * depth], whole)

    if count > 1:
        relayed = functools.reduce(jnp.logical_or, [device == target for target in relays])
        pl.when(relayed)(lambda: multiply(across[1]))
        pl.when(jnp.logical_not(relayed))(lambda: multiply(across[0]))
    else:
        multiply(across[0])
    copy.wait()

    def tile(t, parity):
        m = parity * (blocks // 2) + t // slots
        place = places[(device * blocks + m) * slots + t % slots]
        group, block = place // blocks, jnp.maximum(place, 0) % blocks
        columns = pl.ds(pl.multiple_of(m * width, width), width)
        close = block + jnp.where(group == device, 0, blocks)
        inside = near[pl.ds(pl.multiple_of(close * rows, rows), rows), columns]
        outside = far[pl.ds(pl.multiple_of(block * rows, rows), rows), columns]
        value = jnp.where((group == device) | (group == device ^ 1), inside, outside)
        return jnp.where(place < 0, 0.0, value)

    for t in range(half):
        kept[t * rows : (t + 1) * rows, :] = tile(t, layer % 2)
    encode([tile(t, 1 - layer % 2) for t in range(half)], sent, scales)


def chunk_tiles(relays, pattern, near, whole, across, *earlier):
    blocks, width, _ = whole[0].shape
    rows, slots = across[0].shape[1], pattern.shape[0] // (blocks * lax.axis_size("bas"))
    half = blocks * slots // 2
    return pl.pallas_call(
        functools.partial(tile_kernel, relays, len(across)),
        out_shape=[
            jax.ShapeDtypeStruct((half * rows, width), jnp.float32),
            jax.ShapeDtypeStruct((half * rows + SCALE_ROWS, width), jnp.int16),
        ],
        in_specs=[ANY] + [VMEM] * (1 + PIECES + len(across)) + [ANY] * len(earlier),
        out_specs=[VMEM] * 2,
        scratch_shapes=[
            pltpu.VMEM((blocks * rows, blocks * width), jnp.float32),
            pltpu.VMEM((SCALE_ROWS, width), jnp.float32),
            pltpu.SMEM(pattern.shape, pattern.dtype),
            pltpu.SemaphoreType.DMA,
        ],
        compiler_params=params(24),
        cost_estimate=NO_COST,
    )(pattern, near, *whole, *across, *earlier)


def add_kernel(count, mine, other, coded, scales):
    rows = (coded.shape[0] - SCALE_ROWS) // count
    if mine.dtype == jnp.float32:
        held = [mine[t * rows : (t + 1) * rows, :] for t in range(count)]
    else:
        held = decode(mine, rows, count)
    encode([a + b for a, b in zip(held, decode(other, rows, count))], coded, scales)


def add_coded(count, mine, other):
    return pl.pallas_call(
        functools.partial(add_kernel, count),
        out_shape=jax.ShapeDtypeStruct(other.shape, other.dtype),
        in_specs=[VMEM] * 2,
        out_specs=VMEM,
        scratch_shapes=[pltpu.VMEM((SCALE_ROWS, other.shape[1]), jnp.float32)],
        compiler_params=params(8),
        cost_estimate=NO_COST,
    )(mine, other)


def final_kernel(*refs):
    coded, (out, turned, sems) = refs[:-3], refs[-3:]
    blocks, slots, width, _ = out.shape
    half = blocks * slots // 2
    layer = lax.axis_index("aux")
    copies = []
    for mine in range(2):
        base = jnp.where(layer % 2 == mine, 0, half)
        chunks = [list(decode(part, (part.shape[0] - SCALE_ROWS) // half, half)) for part in coded[mine::2]]
        for t in range(half):
            at = mine * half + t
            turned[at] = jnp.concatenate([chunk[t] for chunk in chunks], axis=0).T
            place = base + t
            copies.append(
                pltpu.make_async_copy(turned.at[at], out.at[place // slots, place % slots], sems.at[at])
            )
            copies[-1].start()
    for copy in copies:
        copy.wait()


def final_tiles(shape, coded):
    blocks, slots, width, _ = shape
    return pl.pallas_call(
        final_kernel,
        out_shape=jax.ShapeDtypeStruct(shape, jnp.float32),
        in_specs=[VMEM] * len(coded),
        out_specs=ANY,
        scratch_shapes=[
            pltpu.VMEM((blocks * slots, width, width), jnp.float32),
            pltpu.SemaphoreType.DMA((blocks * slots,)),
        ],
        compiler_params=params(8),
        cost_estimate=NO_COST,
    )(*coded)


def flipped(size, mask):
    return [(i, i ^ mask) for i in range(size)]


def body(coefficients, tensor, pattern):
    devices, layers = lax.axis_size("bas"), lax.axis_size("aux")
    _, blocks, slots, width, _ = tensor.shape
    chip = flipped(devices, 1)
    across = [pair for i in range(1, devices - 1, 2) for pair in ((i, i + 1), (i + 1, i))]
    detours = ((3, 4, 7), (4, 3, 0)) if devices == 8 else ()
    direct = [pair for pair in across if pair not in [d[:2] for d in detours]]
    there = [(source, via) for source, _, via in detours]
    onward = [(via, target) for _, target, via in detours]
    relays = tuple(target for _, target, _ in detours)

    beyond = lax.ppermute(coefficients, "bas", across)
    beside = lax.ppermute(coefficients, "bas", chip)
    tensor, coefficients = fetch(tensor, coefficients)
    cuts = (0, CUT, width)
    pattern = pattern.reshape(-1)
    (early, late), whole = half_forms(cuts, pattern, coefficients, beside, beyond, tensor)
    arrived = [[lax.ppermute(early, "bas", across)], [lax.ppermute(late, "bas", direct)]]
    if detours:
        arrived[1].append(lax.ppermute(lax.ppermute(late, "bas", there), "bas", onward))
    beside = [lax.ppermute(piece, "bas", chip) for piece in whole]
    half = blocks * slots // 2
    coded, earlier, opened = [], (), gate(arrived[0][0])
    for start, stop, held in zip(cuts, cuts[1:], arrived):
        near = near_products(start, stop, whole, beside, opened)
        kept, sent = chunk_tiles(relays, pattern, near, whole, held, *earlier)
        mine = add_coded(half, kept, lax.ppermute(sent, "aux", flipped(layers, 1)))
        earlier = (mine,)
        mask = 2
        while mask < layers:
            mine = add_coded(half, mine, lax.ppermute(mine, "aux", flipped(layers, mask)))
            mask *= 2
        coded += [mine, lax.ppermute(mine, "aux", flipped(layers, 1))]
    return final_tiles((blocks, slots, width, width), coded)


def solution(mesh):
    return jax.shard_map(
        body,
        mesh=mesh,
        in_specs=(P("bas", None), P("aux", "bas", None, None, None), P()),
        out_specs=P("bas", None, None, None),
        check_vma=False,
    )
```

```python
import functools

import jax
import jax.numpy as jnp
from jax import lax
from jax.experimental import pallas as pl
from jax.experimental.pallas import tpu as pltpu
from jax.sharding import PartitionSpec as P

CUT = 64
PIECES = 2
SCALE_ROWS = 16
FULL = 32752.0
VMEM = pl.BlockSpec(memory_space=pltpu.VMEM)
ANY = pl.BlockSpec(memory_space=pl.ANY)
SMEM = pl.BlockSpec(memory_space=pltpu.SMEM)


def params(mib):
    return pltpu.CompilerParams(vmem_limit_bytes=mib << 20)


NO_COST = pl.CostEstimate(flops=0, bytes_accessed=0, transcendentals=0)


def fetch_kernel(tensor, own, tensor_out, own_out, sems):
    copies = [
        pltpu.make_async_copy(own, own_out, sems.at[0]),
        pltpu.make_async_copy(tensor, tensor_out, sems.at[1]),
    ]
    for copy in copies:
        copy.start()
    for copy in copies:
        copy.wait()


def fetch(tensor, own):
    arrays = (tensor, own)
    return pl.pallas_call(
        fetch_kernel,
        out_shape=[jax.ShapeDtypeStruct(a.shape, a.dtype) for a in arrays],
        in_specs=[ANY] * 2,
        out_specs=[VMEM] * 2,
        scratch_shapes=[pltpu.SemaphoreType.DMA((2,))],
        compiler_params=params(8),
        cost_estimate=NO_COST,
    )(*arrays)


def half_kernel(cuts, pattern, own, beside, across, tensor, *outs):
    parts, pieces = outs[: len(cuts) - 1], outs[len(cuts) - 1 :]
    aux, blocks, slots, width, _ = tensor.shape
    occupied = own.shape[1]
    device = lax.axis_index("bas")
    for m in range(blocks):
        chosen = []
        for j in range(slots):
            place = pattern[(device * blocks + m) * slots + j]
            group = place // blocks
            rows = pl.ds(pl.multiple_of(jnp.maximum(place, 0) % blocks * width, width), width)
            value = jnp.where(group == device ^ 1, beside[rows, :], across[rows, :])
            value = jnp.where(group == device, own[rows, :], value)
            chosen.append(jnp.where(place < 0, jnp.zeros_like(value), value))
        chosen = jnp.concatenate(chosen, axis=0)
        for p in range(aux):
            row = jnp.concatenate([tensor[p, m, j] for j in range(slots)], axis=1)
            half = jnp.dot(row, chosen, preferred_element_type=jnp.float32).astype(jnp.bfloat16)
            piece, column = divmod(p, aux // len(pieces))
            pieces[piece][m, :, column * occupied : (column + 1) * occupied] = half
            for part, start, stop in zip(parts, cuts, cuts[1:]):
                part[m, :, p * occupied : (p + 1) * occupied] = half[start:stop]


def half_forms(cuts, pattern, own, beside, across, tensor):
    aux, blocks, slots, width, _ = tensor.shape
    depth = aux * own.shape[1]
    shapes = [(blocks, b - a, depth) for a, b in zip(cuts, cuts[1:])]
    shapes += [(blocks, width, depth // PIECES)] * PIECES
    outs = pl.pallas_call(
        functools.partial(half_kernel, cuts),
        out_shape=[jax.ShapeDtypeStruct(shape, jnp.bfloat16) for shape in shapes],
        in_specs=[SMEM] + [VMEM] * 4,
        out_specs=[VMEM] * len(shapes),
        compiler_params=params(24),
        cost_estimate=NO_COST,
    )(pattern, own, beside, across, tensor)
    return outs[:-PIECES], outs[-PIECES:]


def encode(tiles, coded, scales):
    rows = tiles[0].shape[0]
    scales[...] = jnp.zeros_like(scales)
    for t, tile in enumerate(tiles):
        most = jnp.max(jnp.abs(tile), axis=0, keepdims=True)
        power = jnp.ceil(jnp.log2(jnp.maximum(most, 2.0**-90)))
        scales[t : t + 1, :] = power
        whole = jnp.round(tile * (FULL * jnp.exp2(-power)))
        coded[t * rows : (t + 1) * rows, :] = whole.astype(jnp.int32).astype(jnp.int16)
    end = len(tiles) * rows
    coded[end : end + SCALE_ROWS, :] = scales[...].astype(jnp.int32).astype(jnp.int16)


def decode(coded, rows, count):
    end = count * rows
    scales = coded[end : end + SCALE_ROWS, :].astype(jnp.int32).astype(jnp.float32)
    scales = jnp.exp2(scales) * (1.0 / FULL)
    for t in range(count):
        value = coded[t * rows : (t + 1) * rows, :].astype(jnp.int32).astype(jnp.float32)
        yield value * scales[t : t + 1, :]


def times(rows, pieces):
    total = 0.0
    for k, piece in enumerate(pieces):
        left, right = rows(k), piece[...]
        total += lax.dot_general(
            left.reshape(-1, left.shape[2]),
            right.reshape(-1, right.shape[2]),
            (((1,), (1,)), ((), ())),
            preferred_element_type=jnp.float32,
        )
    return total


def near_kernel(start, stop, *refs):
    whole, beside, product = refs[:PIECES], refs[PIECES : 2 * PIECES], refs[-1]
    half = product.shape[0] // 2
    product[:half, :] = times(lambda k: whole[k][:, start:stop, :], whole)
    product[half:, :] = times(lambda k: beside[k][:, start:stop, :], whole)


def near_products(start, stop, whole, beside, *earlier):
    blocks, width, _ = whole[0].shape
    return pl.pallas_call(
        functools.partial(near_kernel, start, stop),
        out_shape=jax.ShapeDtypeStruct((2 * blocks * (stop - start), blocks * width), jnp.float32),
        in_specs=[VMEM] * (2 * PIECES) + [ANY] * len(earlier),
        out_specs=VMEM,
        compiler_params=params(24),
        cost_estimate=NO_COST,
    )(*whole, *beside, *earlier)


def gate_kernel(_, out):
    out[...] = jnp.zeros_like(out)


def gate(earlier):
    return pl.pallas_call(
        gate_kernel,
        out_shape=jax.ShapeDtypeStruct((8, 128), jnp.float32),
        in_specs=[ANY],
        out_specs=VMEM,
        compiler_params=params(4),
        cost_estimate=NO_COST,
    )(earlier)


def tile_kernel(relays, count, pattern, near, *refs):
    whole, across, (kept, sent, far, scales, places, sem) = refs[:PIECES], refs[PIECES : PIECES + count], refs[-6:]
    blocks, width, depth = whole[0].shape
    rows = across[0].shape[1]
    slots = pattern.shape[0] // (blocks * lax.axis_size("bas"))
    device, layer = lax.axis_index("bas"), lax.axis_index("aux")
    half = blocks * slots // 2
    copy = pltpu.make_async_copy(pattern, places, sem)
    copy.start()

    def multiply(source):
        far[...] = times(lambda k: source[:, :, k * depth : (k + 1) * depth], whole)

    if count > 1:
        relayed = functools.reduce(jnp.logical_or, [device == target for target in relays])
        pl.when(relayed)(lambda: multiply(across[1]))
        pl.when(jnp.logical_not(relayed))(lambda: multiply(across[0]))
    else:
        multiply(across[0])
    copy.wait()

    def tile(t, parity):
        m = parity * (blocks // 2) + t // slots
        place = places[(device * blocks + m) * slots + t % slots]
        group, block = place // blocks, jnp.maximum(place, 0) % blocks
        columns = pl.ds(pl.multiple_of(m * width, width), width)
        close = block + jnp.where(group == device, 0, blocks)
        inside = near[pl.ds(pl.multiple_of(close * rows, rows), rows), columns]
        outside = far[pl.ds(pl.multiple_of(block * rows, rows), rows), columns]
        value = jnp.where((group == device) | (group == device ^ 1), inside, outside)
        return jnp.where(place < 0, 0.0, value)

    for t in range(half):
        kept[t * rows : (t + 1) * rows, :] = tile(t, layer % 2)
    encode([tile(t, 1 - layer % 2) for t in range(half)], sent, scales)


def chunk_tiles(relays, pattern, near, whole, across, *earlier):
    blocks, width, _ = whole[0].shape
    rows, slots = across[0].shape[1], pattern.shape[0] // (blocks * lax.axis_size("bas"))
    half = blocks * slots // 2
    return pl.pallas_call(
        functools.partial(tile_kernel, relays, len(across)),
        out_shape=[
            jax.ShapeDtypeStruct((half * rows, width), jnp.float32),
            jax.ShapeDtypeStruct((half * rows + SCALE_ROWS, width), jnp.int16),
        ],
        in_specs=[ANY] + [VMEM] * (1 + PIECES + len(across)) + [ANY] * len(earlier),
        out_specs=[VMEM] * 2,
        scratch_shapes=[
            pltpu.VMEM((blocks * rows, blocks * width), jnp.float32),
            pltpu.VMEM((SCALE_ROWS, width), jnp.float32),
            pltpu.SMEM(pattern.shape, pattern.dtype),
            pltpu.SemaphoreType.DMA,
        ],
        compiler_params=params(24),
        cost_estimate=NO_COST,
    )(pattern, near, *whole, *across, *earlier)


def add_kernel(count, mine, other, *rest):
    coded, scales = rest[-2:]
    rows = (coded.shape[0] - SCALE_ROWS) // count
    if mine.dtype == jnp.float32:
        held = [mine[t * rows : (t + 1) * rows, :] for t in range(count)]
    else:
        held = decode(mine, rows, count)
    encode([a + b for a, b in zip(held, decode(other, rows, count))], coded, scales)


def add_coded(count, mine, other, *earlier):
    return pl.pallas_call(
        functools.partial(add_kernel, count),
        out_shape=jax.ShapeDtypeStruct(other.shape, other.dtype),
        in_specs=[VMEM] * 2 + [ANY] * len(earlier),
        out_specs=VMEM,
        scratch_shapes=[pltpu.VMEM((SCALE_ROWS, other.shape[1]), jnp.float32)],
        compiler_params=params(8),
        cost_estimate=NO_COST,
    )(mine, other, *earlier)


def final_kernel(*refs):
    coded, (out, turned, sems) = refs[:-3], refs[-3:]
    blocks, slots, width, _ = out.shape
    half = blocks * slots // 2
    layer = lax.axis_index("aux")
    copies = []
    for mine in range(2):
        base = jnp.where(layer % 2 == mine, 0, half)
        chunks = [list(decode(part, (part.shape[0] - SCALE_ROWS) // half, half)) for part in coded[mine::2]]
        for t in range(half):
            at = mine * half + t
            turned[at] = jnp.concatenate([chunk[t] for chunk in chunks], axis=0).T
            place = base + t
            copies.append(
                pltpu.make_async_copy(turned.at[at], out.at[place // slots, place % slots], sems.at[at])
            )
            copies[-1].start()
    for copy in copies:
        copy.wait()


def final_tiles(shape, coded):
    blocks, slots, width, _ = shape
    return pl.pallas_call(
        final_kernel,
        out_shape=jax.ShapeDtypeStruct(shape, jnp.float32),
        in_specs=[VMEM] * len(coded),
        out_specs=ANY,
        scratch_shapes=[
            pltpu.VMEM((blocks * slots, width, width), jnp.float32),
            pltpu.SemaphoreType.DMA((blocks * slots,)),
        ],
        compiler_params=params(8),
        cost_estimate=NO_COST,
    )(*coded)


def flipped(size, mask):
    return [(i, i ^ mask) for i in range(size)]


def body(coefficients, tensor, pattern):
    devices, layers = lax.axis_size("bas"), lax.axis_size("aux")
    _, blocks, slots, width, _ = tensor.shape
    chip = flipped(devices, 1)
    across = [pair for i in range(1, devices - 1, 2) for pair in ((i, i + 1), (i + 1, i))]
    detours = ((3, 4, 7), (4, 3, 0)) if devices == 8 else ()
    direct = [pair for pair in across if pair not in [d[:2] for d in detours]]
    there = [(source, via) for source, _, via in detours]
    onward = [(via, target) for _, target, via in detours]
    relays = tuple(target for _, target, _ in detours)

    beyond = lax.ppermute(coefficients, "bas", across)
    beside = lax.ppermute(coefficients, "bas", chip)
    tensor, coefficients = fetch(tensor, coefficients)
    cuts = (0, CUT, width)
    pattern = pattern.reshape(-1)
    (early, late), whole = half_forms(cuts, pattern, coefficients, beside, beyond, tensor)
    arrived = [[lax.ppermute(early, "bas", across)], [lax.ppermute(late, "bas", direct)]]
    if detours:
        arrived[1].append(lax.ppermute(lax.ppermute(late, "bas", there), "bas", onward))
    beside = [lax.ppermute(piece, "bas", chip) for piece in whole]
    half = blocks * slots // 2
    coded, earlier, summed, opened = [], (), (), gate(arrived[0][0])
    for start, stop, held in zip(cuts, cuts[1:], arrived):
        near = near_products(start, stop, whole, beside, opened)
        kept, sent = chunk_tiles(relays, pattern, near, whole, held, *earlier)
        mine = add_coded(half, kept, lax.ppermute(sent, "aux", flipped(layers, 1)), *summed)
        earlier = (mine,)
        mask = 2
        while mask < layers:
            mine = add_coded(half, mine, lax.ppermute(mine, "aux", flipped(layers, mask)))
            mask *= 2
        summed = (mine,)
        coded += [mine, lax.ppermute(mine, "aux", flipped(layers, 1))]
    return final_tiles((blocks, slots, width, width), coded)


def solution(mesh):
    return jax.shard_map(
        body,
        mesh=mesh,
        in_specs=(P("bas", None), P("aux", "bas", None, None, None), P()),
        out_specs=P("bas", None, None, None),
        check_vma=False,
    )
```

```python
import functools

import jax
import jax.numpy as jnp
from jax import lax
from jax.experimental import pallas as pl
from jax.experimental.pallas import tpu as pltpu
from jax.sharding import PartitionSpec as P

CUT = 64
PIECES = 2
SCALE_ROWS = 16
FULL = 32752.0
VMEM = pl.BlockSpec(memory_space=pltpu.VMEM)
ANY = pl.BlockSpec(memory_space=pl.ANY)
SMEM = pl.BlockSpec(memory_space=pltpu.SMEM)


def params(mib):
    return pltpu.CompilerParams(vmem_limit_bytes=mib << 20)


NO_COST = pl.CostEstimate(flops=0, bytes_accessed=0, transcendentals=0)


def fetch_kernel(tensor, own, tensor_out, own_out, sems):
    copies = [
        pltpu.make_async_copy(own, own_out, sems.at[0]),
        pltpu.make_async_copy(tensor, tensor_out, sems.at[1]),
    ]
    for copy in copies:
        copy.start()
    for copy in copies:
        copy.wait()


def fetch(tensor, own):
    arrays = (tensor, own)
    return pl.pallas_call(
        fetch_kernel,
        out_shape=[jax.ShapeDtypeStruct(a.shape, a.dtype) for a in arrays],
        in_specs=[ANY] * 2,
        out_specs=[VMEM] * 2,
        scratch_shapes=[pltpu.SemaphoreType.DMA((2,))],
        compiler_params=params(8),
        cost_estimate=NO_COST,
    )(*arrays)


def half_kernel(cuts, pattern, own, across, beside, tensor, *outs):
    parts, pieces = outs[: len(cuts) - 1], outs[len(cuts) - 1 :]
    aux, blocks, slots, width, _ = tensor.shape
    occupied = own.shape[1]
    device = lax.axis_index("bas")
    for m in range(blocks):
        chosen = []
        for j in range(slots):
            place = pattern[(device * blocks + m) * slots + j]
            group = place // blocks
            rows = pl.ds(pl.multiple_of(jnp.maximum(place, 0) % blocks * width, width), width)
            value = jnp.where(group == device ^ 1, beside[rows, :], across[rows, :])
            value = jnp.where(group == device, own[rows, :], value)
            chosen.append(jnp.where(place < 0, jnp.zeros_like(value), value))
        chosen = jnp.concatenate(chosen, axis=0)
        for p in range(aux):
            row = jnp.concatenate([tensor[p, m, j] for j in range(slots)], axis=1)
            half = jnp.dot(row, chosen, preferred_element_type=jnp.float32).astype(jnp.bfloat16)
            piece, column = divmod(p, aux // len(pieces))
            pieces[piece][m, :, column * occupied : (column + 1) * occupied] = half
            for part, start, stop in zip(parts, cuts, cuts[1:]):
                part[m, :, p * occupied : (p + 1) * occupied] = half[start:stop]


def half_forms(cuts, pattern, own, beside, across, tensor):
    aux, blocks, slots, width, _ = tensor.shape
    depth = aux * own.shape[1]
    shapes = [(blocks, b - a, depth) for a, b in zip(cuts, cuts[1:])]
    shapes += [(blocks, width, depth // PIECES)] * PIECES
    outs = pl.pallas_call(
        functools.partial(half_kernel, cuts),
        out_shape=[jax.ShapeDtypeStruct(shape, jnp.bfloat16) for shape in shapes],
        in_specs=[SMEM] + [VMEM] * 4,
        out_specs=[VMEM] * len(shapes),
        compiler_params=params(24),
        cost_estimate=NO_COST,
    )(pattern, own, across, beside, tensor)
    return outs[:-PIECES], outs[-PIECES:]


def encode(tiles, coded, scales):
    rows = tiles[0].shape[0]
    scales[...] = jnp.zeros_like(scales)
    for t, tile in enumerate(tiles):
        most = jnp.max(jnp.abs(tile), axis=0, keepdims=True)
        power = jnp.ceil(jnp.log2(jnp.maximum(most, 2.0**-90)))
        scales[t : t + 1, :] = power
        whole = jnp.round(tile * (FULL * jnp.exp2(-power)))
        coded[t * rows : (t + 1) * rows, :] = whole.astype(jnp.int32).astype(jnp.int16)
    end = len(tiles) * rows
    coded[end : end + SCALE_ROWS, :] = scales[...].astype(jnp.int32).astype(jnp.int16)


def decode(coded, rows, count):
    end = count * rows
    scales = coded[end : end + SCALE_ROWS, :].astype(jnp.int32).astype(jnp.float32)
    scales = jnp.exp2(scales) * (1.0 / FULL)
    for t in range(count):
        value = coded[t * rows : (t + 1) * rows, :].astype(jnp.int32).astype(jnp.float32)
        yield value * scales[t : t + 1, :]


def times(rows, pieces):
    total = 0.0
    for k, piece in enumerate(pieces):
        left, right = rows(k), piece[...]
        total += lax.dot_general(
            left.reshape(-1, left.shape[2]),
            right.reshape(-1, right.shape[2]),
            (((1,), (1,)), ((), ())),
            preferred_element_type=jnp.float32,
        )
    return total


def product_kernel(start, stop, *refs):
    rows, whole, product = refs[:PIECES], refs[PIECES : 2 * PIECES], refs[-1]
    product[...] = times(lambda k: rows[k][:, start:stop, :], whole)


def products(start, stop, rows, whole, *earlier):
    blocks, width, _ = whole[0].shape
    return pl.pallas_call(
        functools.partial(product_kernel, start, stop),
        out_shape=jax.ShapeDtypeStruct((blocks * (stop - start), blocks * width), jnp.float32),
        in_specs=[VMEM] * (2 * PIECES) + [ANY] * len(earlier),
        out_specs=VMEM,
        compiler_params=params(24),
        cost_estimate=NO_COST,
    )(*rows, *whole, *earlier)


def gate_kernel(_, out):
    out[...] = jnp.zeros_like(out)


def gate(earlier):
    return pl.pallas_call(
        gate_kernel,
        out_shape=jax.ShapeDtypeStruct((8, 128), jnp.float32),
        in_specs=[ANY],
        out_specs=VMEM,
        compiler_params=params(4),
        cost_estimate=NO_COST,
    )(earlier)


def tile_kernel(relays, count, start, pattern, own, *refs):
    across, whole, near = refs[:count], refs[count : count + PIECES], refs[count + PIECES : -7]
    kept, sent, far, close, scales, places, sem = refs[-7:]
    blocks, width, depth = whole[0].shape
    rows = across[0].shape[1]
    slots = pattern.shape[0] // (blocks * lax.axis_size("bas"))
    device, layer = lax.axis_index("bas"), lax.axis_index("aux")
    half = blocks * slots // 2
    copy = pltpu.make_async_copy(pattern, places, sem)
    copy.start()

    def multiply(source):
        far[...] = times(lambda k: source[:, :, k * depth : (k + 1) * depth], whole)

    if count > 1:
        relayed = functools.reduce(jnp.logical_or, [device == target for target in relays])
        pl.when(relayed)(lambda: multiply(across[1]))
        pl.when(jnp.logical_not(relayed))(lambda: multiply(across[0]))
    else:
        multiply(across[0])
    if start is None:
        close = near[0]
    else:
        close[...] = times(lambda k: near[k][:, start : start + rows, :], whole)
    copy.wait()

    def tile(t, parity):
        m = parity * (blocks // 2) + t // slots
        place = places[(device * blocks + m) * slots + t % slots]
        group, block = place // blocks, jnp.maximum(place, 0) % blocks
        part = pl.ds(pl.multiple_of(block * rows, rows), rows), pl.ds(pl.multiple_of(m * width, width), width)
        value = jnp.where(group == device ^ 1, close[part], far[part])
        value = jnp.where(group == device, own[part], value)
        return jnp.where(place < 0, 0.0, value)

    for t in range(half):
        kept[t * rows : (t + 1) * rows, :] = tile(t, layer % 2)
    encode([tile(t, 1 - layer % 2) for t in range(half)], sent, scales)


def chunk_tiles(relays, start, pattern, own, across, whole, near, *earlier):
    blocks, width, _ = whole[0].shape
    rows, slots = across[0].shape[1], pattern.shape[0] // (blocks * lax.axis_size("bas"))
    half = blocks * slots // 2
    product = (blocks * rows, blocks * width)

    def kernel(*refs):
        given = 2 + len(across) + len(whole) + len(near)
        tile_kernel(relays, len(across), start, *refs[:given], *refs[given + len(earlier) :])

    return pl.pallas_call(
        kernel,
        out_shape=[
            jax.ShapeDtypeStruct((half * rows, width), jnp.float32),
            jax.ShapeDtypeStruct((half * rows + SCALE_ROWS, width), jnp.int16),
        ],
        in_specs=[ANY] + [VMEM] * (1 + len(across) + len(whole) + len(near)) + [ANY] * len(earlier),
        out_specs=[VMEM] * 2,
        scratch_shapes=[
            pltpu.VMEM(product, jnp.float32),
            pltpu.VMEM((8, 128) if start is None else product, jnp.float32),
            pltpu.VMEM((SCALE_ROWS, width), jnp.float32),
            pltpu.SMEM(pattern.shape, pattern.dtype),
            pltpu.SemaphoreType.DMA,
        ],
        compiler_params=params(24),
        cost_estimate=NO_COST,
    )(pattern, own, *across, *whole, *near, *earlier)


def add_kernel(count, mine, other, *rest):
    coded, scales = rest[-2:]
    rows = (coded.shape[0] - SCALE_ROWS) // count
    if mine.dtype == jnp.float32:
        held = [mine[t * rows : (t + 1) * rows, :] for t in range(count)]
    else:
        held = decode(mine, rows, count)
    encode([a + b for a, b in zip(held, decode(other, rows, count))], coded, scales)


def add_coded(count, mine, other, *earlier):
    return pl.pallas_call(
        functools.partial(add_kernel, count),
        out_shape=jax.ShapeDtypeStruct(other.shape, other.dtype),
        in_specs=[VMEM] * 2 + [ANY] * len(earlier),
        out_specs=VMEM,
        scratch_shapes=[pltpu.VMEM((SCALE_ROWS, other.shape[1]), jnp.float32)],
        compiler_params=params(8),
        cost_estimate=NO_COST,
    )(mine, other, *earlier)


def final_kernel(*refs):
    coded, (out, turned, sems) = refs[:-3], refs[-3:]
    blocks, slots, width, _ = out.shape
    half = blocks * slots // 2
    layer = lax.axis_index("aux")
    copies = []
    for mine in range(2):
        base = jnp.where(layer % 2 == mine, 0, half)
        chunks = [list(decode(part, (part.shape[0] - SCALE_ROWS) // half, half)) for part in coded[mine::2]]
        for t in range(half):
            at = mine * half + t
            turned[at] = jnp.concatenate([chunk[t] for chunk in chunks], axis=0).T
            place = base + t
            copies.append(
                pltpu.make_async_copy(turned.at[at], out.at[place // slots, place % slots], sems.at[at])
            )
            copies[-1].start()
    for copy in copies:
        copy.wait()


def final_tiles(shape, coded):
    blocks, slots, width, _ = shape
    return pl.pallas_call(
        final_kernel,
        out_shape=jax.ShapeDtypeStruct(shape, jnp.float32),
        in_specs=[VMEM] * len(coded),
        out_specs=ANY,
        scratch_shapes=[
            pltpu.VMEM((blocks * slots, width, width), jnp.float32),
            pltpu.SemaphoreType.DMA((blocks * slots,)),
        ],
        compiler_params=params(8),
        cost_estimate=NO_COST,
    )(*coded)


def flipped(size, mask):
    return [(i, i ^ mask) for i in range(size)]


def body(coefficients, tensor, pattern):
    devices, layers = lax.axis_size("bas"), lax.axis_size("aux")
    _, blocks, slots, width, _ = tensor.shape
    chip = flipped(devices, 1)
    across = [pair for i in range(1, devices - 1, 2) for pair in ((i, i + 1), (i + 1, i))]
    detours = ((3, 4, 7), (4, 3, 0)) if devices == 8 else ()
    direct = [pair for pair in across if pair not in [d[:2] for d in detours]]
    there = [(source, via) for source, _, via in detours]
    onward = [(via, target) for _, target, via in detours]
    relays = tuple(target for _, target, _ in detours)

    beyond = lax.ppermute(coefficients, "bas", across)
    beside = lax.ppermute(coefficients, "bas", chip)
    tensor, coefficients = fetch(tensor, coefficients)
    cuts = (0, CUT, width)
    pattern = pattern.reshape(-1)
    (early, *late), whole = half_forms(cuts, pattern, coefficients, beside, beyond, tensor)
    arrived = [[lax.ppermute(early, "bas", across)]] + [[lax.ppermute(part, "bas", direct)] for part in late]
    if detours:
        halfway = [lax.ppermute(part, "bas", there) for part in late]
        for held, part in zip(arrived[1:], halfway):
            held.append(lax.ppermute(part, "bas", onward))
    beside = [lax.ppermute(piece, "bas", chip) for piece in whole]
    half = blocks * slots // 2
    opened = gate(arrived[0][0])
    owned = [products(a, b, whole, whole, halfway[-1] if detours else opened) for a, b in zip(cuts, cuts[1:])]
    coded, earlier, summed = [], (opened,), ()
    for start, stop, own, held in zip(cuts, cuts[1:], owned, arrived):
        if start == 0:
            kept, sent = chunk_tiles(relays, 0, pattern, own, held, whole, beside, *earlier)
        else:
            near = products(start, stop, beside, whole, opened)
            kept, sent = chunk_tiles(relays, None, pattern, own, held, whole, [near], *earlier)
        mine = add_coded(half, kept, lax.ppermute(sent, "aux", flipped(layers, 1)), *summed)
        earlier = (mine,)
        mask = 2
        while mask < layers:
            mine = add_coded(half, mine, lax.ppermute(mine, "aux", flipped(layers, mask)))
            mask *= 2
        summed = (mine,)
        coded += [mine, lax.ppermute(mine, "aux", flipped(layers, 1))]
    return final_tiles((blocks, slots, width, width), coded)


def solution(mesh):
    return jax.shard_map(
        body,
        mesh=mesh,
        in_specs=(P("bas", None), P("aux", "bas", None, None, None), P()),
        out_specs=P("bas", None, None, None),
        check_vma=False,
    )
```

```python
import functools
import itertools

import jax
import jax.numpy as jnp
import numpy as np
from jax import lax
from jax.experimental import pallas as pl
from jax.experimental.pallas import tpu as pltpu
from jax.sharding import PartitionSpec as P

CUT = 64
FEW = 3
SCALE_ROWS = 16
FULL = 32752.0
VMEM = pl.BlockSpec(memory_space=pltpu.VMEM)
ANY = pl.BlockSpec(memory_space=pl.ANY)
SMEM = pl.BlockSpec(memory_space=pltpu.SMEM)


def params(mib):
    return pltpu.CompilerParams(vmem_limit_bytes=mib << 20)


NO_COST = pl.CostEstimate(flops=0, bytes_accessed=0, transcendentals=0)


def piece_sizes(aux, count):
    return [aux // count + (k < aux % count) for k in range(count)]


def neighbour(device):
    return device + 2 * (device % 2) - 1


def most_needed(pattern, devices):
    rows = np.arange(pattern.shape[1])
    blocks = len(rows) // devices
    other = neighbour(np.arange(devices))
    wanted = other[:, None] * blocks + np.arange(blocks)
    wanted = np.where(((other >= 0) & (other < devices))[:, None], wanted, -2).astype(np.int32)
    own = rows // blocks == np.arange(devices)[:, None]
    listed = (pattern == wanted[:, :, None, None]) & own[:, None, None, :]
    return jnp.max(jnp.sum(jnp.any(listed, axis=(2, 3)), axis=1))


def needed(pattern, blocks, of, by):
    listed = [pattern[j, by * blocks + m] for j in range(pattern.shape[0]) for m in range(blocks)]
    return [functools.reduce(jnp.logical_or, [one == of * blocks + block for one in listed]) for block in range(blocks)]


def fetch_kernel(tensor, own, tensor_out, own_out, sems):
    copies = [
        pltpu.make_async_copy(own, own_out, sems.at[0]),
        pltpu.make_async_copy(tensor, tensor_out, sems.at[1]),
    ]
    for copy in copies:
        copy.start()
    for copy in copies:
        copy.wait()


def fetch(tensor, own):
    arrays = (tensor, own)
    return pl.pallas_call(
        fetch_kernel,
        out_shape=[jax.ShapeDtypeStruct(a.shape, a.dtype) for a in arrays],
        in_specs=[ANY] * 2,
        out_specs=[VMEM] * 2,
        scratch_shapes=[pltpu.SemaphoreType.DMA((2,))],
        compiler_params=params(8),
        cost_estimate=NO_COST,
    )(*(pltpu.with_memory_space_constraint(a, pltpu.HBM) for a in arrays))


def half_kernel(cuts, count, relays, pattern, own, *refs):
    outs = refs[-(len(cuts) - 1 + count) :]
    parts, pieces = outs[: len(cuts) - 1], outs[len(cuts) - 1 :]
    *across, beside, tensor = refs[: -len(outs)]
    aux, blocks, slots, width, _ = tensor.shape
    occupied = own.shape[1]
    sizes = piece_sizes(aux, count)
    owner = [(k, i) for k, size in enumerate(sizes) for i in range(size)]
    device = lax.axis_index("bas")
    relayed = functools.reduce(jnp.logical_or, [device == target for target in relays], False)
    held = parts[0].shape[0]
    other = neighbour(device)
    there = (other >= 0) & (other < lax.axis_size("bas"))
    if held < blocks:
        asked = needed(pattern, blocks, device, jnp.clip(other, 0, lax.axis_size("bas") - 1))
    packed = jnp.int32(0)
    for m in range(blocks):
        chosen = []
        for j in range(slots):
            place = pattern[j, device * blocks + m]
            group = place // blocks
            rows = pl.ds(pl.multiple_of(jnp.maximum(place, 0) % blocks * width, width), width)
            value = across[0][rows, :]
            if relays:
                value = jnp.where(relayed, across[1][rows, :], value)
            value = jnp.where(group == device ^ 1, beside[rows, :], value)
            value = jnp.where(group == device, own[rows, :], value)
            chosen.append(jnp.where(place < 0, jnp.zeros_like(value), value))
        chosen = jnp.concatenate(chosen, axis=0)
        for p in range(aux):
            row = jnp.concatenate([tensor[p, m, j] for j in range(slots)], axis=1)
            half = jnp.dot(row, chosen, preferred_element_type=jnp.float32).astype(jnp.bfloat16)
            piece, column = owner[p]
            pieces[piece][m, :, column * occupied : (column + 1) * occupied] = half
            for part, start, stop in zip(parts, cuts, cuts[1:]):
                if held == blocks:
                    part[m, :, p * occupied : (p + 1) * occupied] = half[start:stop]
                elif m < held:
                    part[packed, :, p * occupied : (p + 1) * occupied] = half[start:stop]
        if held <= m:

            @pl.when(packed < held)
            def _():
                for part, start, stop in zip(parts, cuts, cuts[1:]):
                    at = 0
                    for piece in pieces:
                        part[packed, :, at : at + piece.shape[2]] = piece[m, start:stop, :]
                        at += piece.shape[2]

        if held < blocks:
            packed += (asked[m] & there).astype(jnp.int32)


def half_forms(held, count, cuts, relays, pattern, own, beside, across, tensor):
    aux, blocks, slots, width, _ = tensor.shape
    depth = aux * own.shape[1]
    shapes = [(held, b - a, depth) for a, b in zip(cuts, cuts[1:])]
    shapes += [(blocks, width, size * own.shape[1]) for size in piece_sizes(aux, count)]
    outs = pl.pallas_call(
        functools.partial(half_kernel, cuts, count, relays),
        out_shape=[jax.ShapeDtypeStruct(shape, jnp.bfloat16) for shape in shapes],
        in_specs=[SMEM] + [VMEM] * (3 + len(across)),
        out_specs=[VMEM] * len(shapes),
        compiler_params=params(24),
        cost_estimate=NO_COST,
    )(pattern, own, *across, beside, tensor)
    return outs[:-count], outs[-count:]


def encode(tiles, coded, scales):
    rows = tiles[0].shape[0]
    scales[...] = jnp.zeros_like(scales)
    for t, tile in enumerate(tiles):
        most = jnp.max(jnp.abs(tile), axis=0, keepdims=True)
        power = jnp.ceil(jnp.log2(jnp.maximum(most, 2.0**-90)))
        scales[t : t + 1, :] = power
        whole = jnp.round(tile * (FULL * jnp.exp2(-power)))
        coded[t * rows : (t + 1) * rows, :] = whole.astype(jnp.int32).astype(jnp.int16)
    end = len(tiles) * rows
    coded[end : end + SCALE_ROWS, :] = scales[...].astype(jnp.int32).astype(jnp.int16)


def decode(coded, rows, count):
    end = count * rows
    scales = coded[end : end + SCALE_ROWS, :].astype(jnp.int32).astype(jnp.float32)
    scales = jnp.exp2(scales) * (1.0 / FULL)
    for t in range(count):
        value = coded[t * rows : (t + 1) * rows, :].astype(jnp.int32).astype(jnp.float32)
        yield value * scales[t : t + 1, :]


def times(rows, pieces):
    total = 0.0
    for k, piece in enumerate(pieces):
        left, right = rows(k), piece[...]
        total += lax.dot_general(
            left.reshape(-1, left.shape[2]),
            right.reshape(-1, right.shape[2]),
            (((1,), (1,)), ((), ())),
            preferred_element_type=jnp.float32,
        )
    return total


def product_kernel(count, start, stop, *refs):
    rows, whole, product = refs[:count], refs[count : 2 * count], refs[-1]
    product[...] = times(lambda k: rows[k][:, start:stop, :], whole)


def products(start, stop, rows, whole, *earlier):
    blocks, width, _ = whole[0].shape
    return pl.pallas_call(
        functools.partial(product_kernel, len(whole), start, stop),
        out_shape=jax.ShapeDtypeStruct((blocks * (stop - start), blocks * width), jnp.float32),
        in_specs=[VMEM] * (2 * len(whole)) + [ANY] * len(earlier),
        out_specs=VMEM,
        compiler_params=params(24),
        cost_estimate=NO_COST,
    )(*rows, *whole, *earlier)


def gate_kernel(_, out):
    out[...] = jnp.zeros_like(out)


def gate(earlier):
    return pl.pallas_call(
        gate_kernel,
        out_shape=jax.ShapeDtypeStruct((8, 128), jnp.float32),
        in_specs=[ANY],
        out_specs=VMEM,
        compiler_params=params(4),
        cost_estimate=NO_COST,
    )(earlier)


def tile_kernel(relays, count, pieces, start, pattern, own, *refs):
    across, whole, near = refs[:count], refs[count : count + pieces], refs[count + pieces : -7]
    kept, sent, far, close, scales, places, sem = refs[-7:]
    blocks, width, _ = whole[0].shape
    ends = list(itertools.accumulate([piece.shape[2] for piece in whole], initial=0))
    rows = across[0].shape[1]
    slots = pattern.shape[0]
    device, layer = lax.axis_index("bas"), lax.axis_index("aux")
    half = blocks * slots // 2
    copy = pltpu.make_async_copy(pattern, places, sem)
    copy.start()

    def multiply(source):
        far[...] = times(lambda k: source[:, :, ends[k] : ends[k + 1]], whole)

    if count > 1:
        relayed = functools.reduce(jnp.logical_or, [device == target for target in relays])
        pl.when(relayed)(lambda: multiply(across[1]))
        pl.when(jnp.logical_not(relayed))(lambda: multiply(across[0]))
    else:
        multiply(across[0])
    if start is None:
        close = near[0]
    else:
        close[...] = times(lambda k: near[k][:, start : start + rows, :], whole)
    copy.wait()
    held = far.shape[0] // rows
    if held < blocks:
        asked = needed(places, blocks, neighbour(device), device)

    def tile(t, parity):
        m = parity * (blocks // 2) + t // slots
        place = places[t % slots, device * blocks + m]
        group, block = place // blocks, jnp.maximum(place, 0) % blocks
        columns = pl.ds(pl.multiple_of(m * width, width), width)
        part = pl.ds(pl.multiple_of(block * rows, rows), rows), columns
        if held < blocks:
            before = [jnp.where(asked[i] & (i < block), 1, 0) for i in range(blocks)]
            block = jnp.minimum(sum(before), held - 1)
        value = far[pl.ds(pl.multiple_of(block * rows, rows), rows), columns]
        value = jnp.where(group == device ^ 1, close[part], value)
        value = jnp.where(group == device, own[part], value)
        return jnp.where(place < 0, 0.0, value)

    for t in range(half):
        kept[t * rows : (t + 1) * rows, :] = tile(t, layer % 2)
    encode([tile(t, 1 - layer % 2) for t in range(half)], sent, scales)


def chunk_tiles(relays, start, pattern, own, across, whole, near, *earlier):
    blocks, width, _ = whole[0].shape
    rows, slots = across[0].shape[1], pattern.shape[0]
    half = blocks * slots // 2
    product = (blocks * rows, blocks * width)
    held = across[0].shape[0]

    def kernel(*refs):
        given = 2 + len(across) + len(whole) + len(near)
        tile_kernel(relays, len(across), len(whole), start, *refs[:given], *refs[given + len(earlier) :])

    return pl.pallas_call(
        kernel,
        out_shape=[
            jax.ShapeDtypeStruct((half * rows, width), jnp.float32),
            jax.ShapeDtypeStruct((half * rows + SCALE_ROWS, width), jnp.int16),
        ],
        in_specs=[ANY] + [VMEM] * (1 + len(across) + len(whole) + len(near)) + [ANY] * len(earlier),
        out_specs=[VMEM] * 2,
        scratch_shapes=[
            pltpu.VMEM((held * rows, blocks * width), jnp.float32),
            pltpu.VMEM((8, 128) if start is None else product, jnp.float32),
            pltpu.VMEM((SCALE_ROWS, width), jnp.float32),
            pltpu.SMEM(pattern.shape, pattern.dtype),
            pltpu.SemaphoreType.DMA,
        ],
        compiler_params=params(24),
        cost_estimate=NO_COST,
    )(pattern, own, *across, *whole, *near, *earlier)


def add_kernel(count, mine, other, *rest):
    coded, scales = rest[-2:]
    rows = (coded.shape[0] - SCALE_ROWS) // count
    if mine.dtype == jnp.float32:
        held = [mine[t * rows : (t + 1) * rows, :] for t in range(count)]
    else:
        held = decode(mine, rows, count)
    encode([a + b for a, b in zip(held, decode(other, rows, count))], coded, scales)


def add_coded(count, mine, other, *earlier):
    return pl.pallas_call(
        functools.partial(add_kernel, count),
        out_shape=jax.ShapeDtypeStruct(other.shape, other.dtype),
        in_specs=[VMEM] * 2 + [ANY] * len(earlier),
        out_specs=VMEM,
        scratch_shapes=[pltpu.VMEM((SCALE_ROWS, other.shape[1]), jnp.float32)],
        compiler_params=params(8),
        cost_estimate=NO_COST,
    )(mine, other, *earlier)


def final_kernel(*refs):
    coded, out = refs[:-1], refs[-1]
    blocks, slots, width, _ = out.shape
    half = blocks * slots // 2
    layer = lax.axis_index("aux")
    for mine in range(2):
        base = jnp.where(layer % 2 == mine, 0, half)
        chunks = [list(decode(part, (part.shape[0] - SCALE_ROWS) // half, half)) for part in coded[mine::2]]
        for t in range(half):
            place = base + t
            out[place // slots, place % slots] = jnp.concatenate([chunk[t] for chunk in chunks], axis=0).T


def final_tiles(shape, coded):
    return pl.pallas_call(
        final_kernel,
        out_shape=jax.ShapeDtypeStruct(shape, jnp.float32),
        in_specs=[VMEM] * len(coded),
        out_specs=VMEM,
        compiler_params=params(8),
        cost_estimate=NO_COST,
    )(*coded)


def flipped(size, mask):
    return [(i, i ^ mask) for i in range(size)]


def body(coefficients, tensor, pattern):
    devices, layers = lax.axis_size("bas"), lax.axis_size("aux")
    _, blocks, slots, width, _ = tensor.shape
    chip = flipped(devices, 1)
    across = [pair for i in range(1, devices - 1, 2) for pair in ((i, i + 1), (i + 1, i))]
    detours = ((3, 4, 7), (4, 3, 0)) if devices == 8 else ()
    direct = [pair for pair in across if pair not in [d[:2] for d in detours]]
    there = [(source, via) for source, _, via in detours]
    onward = [(via, target) for _, target, via in detours]
    relays = tuple(target for _, target, _ in detours)

    beyond = [lax.ppermute(coefficients, "bas", direct)]
    if detours:
        beyond.append(lax.ppermute(coefficients, "bas", [pair for pair in across if pair not in direct]))
    beside = lax.ppermute(coefficients, "bas", chip)
    tensor, coefficients = fetch(tensor, coefficients)
    cuts = (0, CUT, width)
    pattern = pattern.T
    few = most_needed(pattern, devices) <= FEW

    def exchange(held, count, pattern, coefficients, beside, beyond, tensor):
        (early, *late), whole = half_forms(held, count, cuts, relays, pattern, coefficients, beside, beyond, tensor)
        arrived = [[lax.ppermute(early, "bas", across)]] + [[lax.ppermute(part, "bas", direct)] for part in late]
        if detours:
            halfway = [lax.ppermute(part, "bas", there) for part in late]
            for got, part in zip(arrived[1:], halfway):
                got.append(lax.ppermute(part, "bas", onward))
        beside = [lax.ppermute(piece, "bas", chip) for piece in whole]
        half = blocks * slots // 2
        opened = gate(arrived[0][0])
        owned = [products(a, b, whole, whole, halfway[-1] if detours else opened) for a, b in zip(cuts, cuts[1:])]
        coded, earlier, summed = [], (opened,), ()
        for start, stop, own, got in zip(cuts, cuts[1:], owned, arrived):
            if start == 0:
                kept, sent = chunk_tiles(relays, 0, pattern, own, got, whole, beside, *earlier)
            else:
                near = products(start, stop, beside, whole, opened)
                kept, sent = chunk_tiles(relays, None, pattern, own, got, whole, [near], *earlier)
            mine = add_coded(half, kept, lax.ppermute(sent, "aux", flipped(layers, 1)), *summed)
            earlier = (mine,)
            mask = 2
            while mask < layers:
                mine = add_coded(half, mine, lax.ppermute(mine, "aux", flipped(layers, mask)))
                mask *= 2
            summed = (mine,)
            coded += [mine, lax.ppermute(mine, "aux", flipped(layers, 1))]
        return final_tiles((blocks, slots, width, width), coded)

    operands = (pattern, coefficients, beside, beyond, tensor)
    if blocks <= FEW:
        return exchange(blocks, 2, *operands)
    return lax.cond(few, functools.partial(exchange, FEW, 2), functools.partial(exchange, blocks, 2), *operands)


def solution(mesh):
    return jax.shard_map(
        body,
        mesh=mesh,
        in_specs=(P("bas", None), P("aux", "bas", None, None, None), P()),
        out_specs=P("bas", None, None, None),
        check_vma=False,
    )
```

```python
import functools
import itertools

import jax
import jax.numpy as jnp
import numpy as np
from jax import lax
from jax.experimental import pallas as pl
from jax.experimental.pallas import tpu as pltpu
from jax.sharding import PartitionSpec as P

CUT = 64
FEW = 3
SCALE_ROWS = 16
FULL = 32752.0
VMEM = pl.BlockSpec(memory_space=pltpu.VMEM)
ANY = pl.BlockSpec(memory_space=pl.ANY)
SMEM = pl.BlockSpec(memory_space=pltpu.SMEM)


def params(mib):
    return pltpu.CompilerParams(vmem_limit_bytes=mib << 20)


NO_COST = pl.CostEstimate(flops=0, bytes_accessed=0, transcendentals=0)
LONG = pl.CostEstimate(flops=6 * 10**9, bytes_accessed=0, transcendentals=0)


def piece_sizes(aux, count):
    return [aux // count + (k < aux % count) for k in range(count)]


def neighbour(device):
    return device + 2 * (device % 2) - 1


def most_needed(pattern, devices):
    rows = np.arange(pattern.shape[1])
    blocks = len(rows) // devices
    other = neighbour(np.arange(devices))
    wanted = other[:, None] * blocks + np.arange(blocks)
    wanted = np.where(((other >= 0) & (other < devices))[:, None], wanted, -2).astype(np.int32)
    own = rows // blocks == np.arange(devices)[:, None]
    listed = (pattern == wanted[:, :, None, None]) & own[:, None, None, :]
    return jnp.max(jnp.sum(jnp.any(listed, axis=(2, 3)), axis=1))


def needed(pattern, blocks, of, by):
    listed = [pattern[j, by * blocks + m] for j in range(pattern.shape[0]) for m in range(blocks)]
    return [functools.reduce(jnp.logical_or, [one == of * blocks + block for one in listed]) for block in range(blocks)]


def fetch_kernel(tensor, own, tensor_out, own_out, sems):
    copies = [
        pltpu.make_async_copy(own, own_out, sems.at[0]),
        pltpu.make_async_copy(tensor, tensor_out, sems.at[1]),
    ]
    for copy in copies:
        copy.start()
    for copy in copies:
        copy.wait()


def fetch(tensor, own):
    arrays = (tensor, own)
    return pl.pallas_call(
        fetch_kernel,
        out_shape=[jax.ShapeDtypeStruct(a.shape, a.dtype) for a in arrays],
        in_specs=[ANY] * 2,
        out_specs=[VMEM] * 2,
        scratch_shapes=[pltpu.SemaphoreType.DMA((2,))],
        compiler_params=params(8),
        cost_estimate=NO_COST,
    )(*(pltpu.with_memory_space_constraint(a, pltpu.HBM) for a in arrays))


def half_kernel(cuts, count, relays, pattern, own, *refs):
    outs = refs[-(len(cuts) - 1 + count) :]
    parts, pieces = outs[: len(cuts) - 1], outs[len(cuts) - 1 :]
    *across, beside, tensor = refs[: -len(outs)]
    aux, blocks, slots, width, _ = tensor.shape
    occupied = own.shape[1]
    sizes = piece_sizes(aux, count)
    owner = [(k, i) for k, size in enumerate(sizes) for i in range(size)]
    device = lax.axis_index("bas")
    relayed = functools.reduce(jnp.logical_or, [device == target for target in relays], False)
    held = parts[0].shape[0]
    other = neighbour(device)
    there = (other >= 0) & (other < lax.axis_size("bas"))
    if held < blocks:
        asked = needed(pattern, blocks, device, jnp.clip(other, 0, lax.axis_size("bas") - 1))
    packed = jnp.int32(0)
    for m in range(blocks):
        chosen = []
        for j in range(slots):
            place = pattern[j, device * blocks + m]
            group = place // blocks
            rows = pl.ds(pl.multiple_of(jnp.maximum(place, 0) % blocks * width, width), width)
            value = across[0][rows, :]
            if relays:
                value = jnp.where(relayed, across[1][rows, :], value)
            value = jnp.where(group == device ^ 1, beside[rows, :], value)
            value = jnp.where(group == device, own[rows, :], value)
            chosen.append(jnp.where(place < 0, jnp.zeros_like(value), value))
        chosen = jnp.concatenate(chosen, axis=0)
        for p in range(aux):
            row = jnp.concatenate([tensor[p, m, j] for j in range(slots)], axis=1)
            half = jnp.dot(row, chosen, preferred_element_type=jnp.float32).astype(jnp.bfloat16)
            piece, column = owner[p]
            pieces[piece][m, :, column * occupied : (column + 1) * occupied] = half
            for part, start, stop in zip(parts, cuts, cuts[1:]):
                if held == blocks:
                    part[m, :, p * occupied : (p + 1) * occupied] = half[start:stop]
                elif m < held:
                    part[packed, :, p * occupied : (p + 1) * occupied] = half[start:stop]
        if held <= m:

            @pl.when(packed < held)
            def _():
                for part, start, stop in zip(parts, cuts, cuts[1:]):
                    at = 0
                    for piece in pieces:
                        part[packed, :, at : at + piece.shape[2]] = piece[m, start:stop, :]
                        at += piece.shape[2]

        if held < blocks:
            packed += (asked[m] & there).astype(jnp.int32)


def half_forms(held, count, cuts, relays, pattern, own, beside, across, tensor):
    aux, blocks, slots, width, _ = tensor.shape
    depth = aux * own.shape[1]
    shapes = [(held, b - a, depth) for a, b in zip(cuts, cuts[1:])]
    shapes += [(blocks, width, size * own.shape[1]) for size in piece_sizes(aux, count)]
    outs = pl.pallas_call(
        functools.partial(half_kernel, cuts, count, relays),
        out_shape=[jax.ShapeDtypeStruct(shape, jnp.bfloat16) for shape in shapes],
        in_specs=[SMEM] + [VMEM] * (3 + len(across)),
        out_specs=[VMEM] * len(shapes),
        compiler_params=params(24),
        cost_estimate=NO_COST,
    )(pattern, own, *across, beside, tensor)
    return outs[:-count], outs[-count:]


def encode(tiles, coded, scales):
    rows = tiles[0].shape[0]
    scales[...] = jnp.zeros_like(scales)
    for t, tile in enumerate(tiles):
        most = jnp.max(jnp.abs(tile), axis=0, keepdims=True)
        power = jnp.ceil(jnp.log2(jnp.maximum(most, 2.0**-90)))
        scales[t : t + 1, :] = power
        whole = jnp.round(tile * (FULL * jnp.exp2(-power)))
        coded[t * rows : (t + 1) * rows, :] = whole.astype(jnp.int32).astype(jnp.int16)
    end = len(tiles) * rows
    coded[end : end + SCALE_ROWS, :] = scales[...].astype(jnp.int32).astype(jnp.int16)


def decode(coded, rows, count):
    end = count * rows
    scales = coded[end : end + SCALE_ROWS, :].astype(jnp.int32).astype(jnp.float32)
    scales = jnp.exp2(scales) * (1.0 / FULL)
    for t in range(count):
        value = coded[t * rows : (t + 1) * rows, :].astype(jnp.int32).astype(jnp.float32)
        yield value * scales[t : t + 1, :]


def times(rows, pieces):
    total = 0.0
    for k, piece in enumerate(pieces):
        left, right = rows(k), piece[...]
        total += lax.dot_general(
            left.reshape(-1, left.shape[2]),
            right.reshape(-1, right.shape[2]),
            (((1,), (1,)), ((), ())),
            preferred_element_type=jnp.float32,
        )
    return total


def product_kernel(count, start, stop, *refs):
    rows, whole, product = refs[:count], refs[count : 2 * count], refs[-1]
    product[...] = times(lambda k: rows[k][:, start:stop, :], whole)


def products(start, stop, rows, whole, *earlier):
    blocks, width, _ = whole[0].shape
    return pl.pallas_call(
        functools.partial(product_kernel, len(whole), start, stop),
        out_shape=jax.ShapeDtypeStruct((blocks * (stop - start), blocks * width), jnp.float32),
        in_specs=[VMEM] * (2 * len(whole)) + [ANY] * len(earlier),
        out_specs=VMEM,
        compiler_params=params(24),
        cost_estimate=NO_COST,
    )(*rows, *whole, *earlier)


def gate_kernel(_, out):
    out[...] = jnp.zeros_like(out)


def gate(earlier):
    return pl.pallas_call(
        gate_kernel,
        out_shape=jax.ShapeDtypeStruct((8, 128), jnp.float32),
        in_specs=[ANY],
        out_specs=VMEM,
        compiler_params=params(4),
        cost_estimate=LONG,
    )(earlier)


def tile_kernel(relays, count, pieces, start, pattern, own, *refs):
    across, whole, near = refs[:count], refs[count : count + pieces], refs[count + pieces : -7]
    kept, sent, far, close, scales, places, sem = refs[-7:]
    blocks, width, _ = whole[0].shape
    ends = list(itertools.accumulate([piece.shape[2] for piece in whole], initial=0))
    rows = across[0].shape[1]
    slots = pattern.shape[0]
    device, layer = lax.axis_index("bas"), lax.axis_index("aux")
    half = blocks * slots // 2
    copy = pltpu.make_async_copy(pattern, places, sem)
    copy.start()

    def multiply(source):
        far[...] = times(lambda k: source[:, :, ends[k] : ends[k + 1]], whole)

    if count > 1:
        relayed = functools.reduce(jnp.logical_or, [device == target for target in relays])
        pl.when(relayed)(lambda: multiply(across[1]))
        pl.when(jnp.logical_not(relayed))(lambda: multiply(across[0]))
    else:
        multiply(across[0])
    if start is None:
        close = near[0]
    else:
        close[...] = times(lambda k: near[k][:, start : start + rows, :], whole)
    copy.wait()
    held = far.shape[0] // rows
    if held < blocks:
        asked = needed(places, blocks, neighbour(device), device)

    def tile(t, parity):
        m = parity * (blocks // 2) + t // slots
        place = places[t % slots, device * blocks + m]
        group, block = place // blocks, jnp.maximum(place, 0) % blocks
        columns = pl.ds(pl.multiple_of(m * width, width), width)
        part = pl.ds(pl.multiple_of(block * rows, rows), rows), columns
        if held < blocks:
            before = [jnp.where(asked[i] & (i < block), 1, 0) for i in range(blocks)]
            block = jnp.minimum(sum(before), held - 1)
        value = far[pl.ds(pl.multiple_of(block * rows, rows), rows), columns]
        value = jnp.where(group == device ^ 1, close[part], value)
        value = jnp.where(group == device, own[part], value)
        return jnp.where(place < 0, 0.0, value)

    for t in range(half):
        kept[t * rows : (t + 1) * rows, :] = tile(t, layer % 2)
    encode([tile(t, 1 - layer % 2) for t in range(half)], sent, scales)


def chunk_tiles(relays, start, pattern, own, across, whole, near, *earlier):
    blocks, width, _ = whole[0].shape
    rows, slots = across[0].shape[1], pattern.shape[0]
    half = blocks * slots // 2
    product = (blocks * rows, blocks * width)
    held = across[0].shape[0]

    def kernel(*refs):
        given = 2 + len(across) + len(whole) + len(near)
        tile_kernel(relays, len(across), len(whole), start, *refs[:given], *refs[given + len(earlier) :])

    return pl.pallas_call(
        kernel,
        out_shape=[
            jax.ShapeDtypeStruct((half * rows, width), jnp.float32),
            jax.ShapeDtypeStruct((half * rows + SCALE_ROWS, width), jnp.int16),
        ],
        in_specs=[ANY] + [VMEM] * (1 + len(across) + len(whole) + len(near)) + [ANY] * len(earlier),
        out_specs=[VMEM] * 2,
        scratch_shapes=[
            pltpu.VMEM((held * rows, blocks * width), jnp.float32),
            pltpu.VMEM((8, 128) if start is None else product, jnp.float32),
            pltpu.VMEM((SCALE_ROWS, width), jnp.float32),
            pltpu.SMEM(pattern.shape, pattern.dtype),
            pltpu.SemaphoreType.DMA,
        ],
        compiler_params=params(24),
        cost_estimate=NO_COST,
    )(pattern, own, *across, *whole, *near, *earlier)


def add_kernel(count, mine, other, *rest):
    coded, scales = rest[-2:]
    rows = (coded.shape[0] - SCALE_ROWS) // count
    if mine.dtype == jnp.float32:
        held = [mine[t * rows : (t + 1) * rows, :] for t in range(count)]
    else:
        held = decode(mine, rows, count)
    encode([a + b for a, b in zip(held, decode(other, rows, count))], coded, scales)


def add_coded(count, mine, other, *earlier):
    return pl.pallas_call(
        functools.partial(add_kernel, count),
        out_shape=jax.ShapeDtypeStruct(other.shape, other.dtype),
        in_specs=[VMEM] * 2 + [ANY] * len(earlier),
        out_specs=VMEM,
        scratch_shapes=[pltpu.VMEM((SCALE_ROWS, other.shape[1]), jnp.float32)],
        compiler_params=params(8),
        cost_estimate=NO_COST,
    )(mine, other, *earlier)


def final_kernel(*refs):
    coded, out = refs[:-1], refs[-1]
    blocks, slots, width, _ = out.shape
    half = blocks * slots // 2
    layer = lax.axis_index("aux")
    for mine in range(2):
        base = jnp.where(layer % 2 == mine, 0, half)
        chunks = [list(decode(part, (part.shape[0] - SCALE_ROWS) // half, half)) for part in coded[mine::2]]
        for t in range(half):
            place = base + t
            out[place // slots, place % slots] = jnp.concatenate([chunk[t] for chunk in chunks], axis=0).T


def final_tiles(shape, coded):
    return pl.pallas_call(
        final_kernel,
        out_shape=jax.ShapeDtypeStruct(shape, jnp.float32),
        in_specs=[VMEM] * len(coded),
        out_specs=VMEM,
        compiler_params=params(8),
        cost_estimate=NO_COST,
    )(*coded)


def flipped(size, mask):
    return [(i, i ^ mask) for i in range(size)]


def body(coefficients, tensor, pattern):
    devices, layers = lax.axis_size("bas"), lax.axis_size("aux")
    _, blocks, slots, width, _ = tensor.shape
    chip = flipped(devices, 1)
    across = [pair for i in range(1, devices - 1, 2) for pair in ((i, i + 1), (i + 1, i))]
    detours = ((3, 4, 7), (4, 3, 0)) if devices == 8 else ()
    direct = [pair for pair in across if pair not in [d[:2] for d in detours]]
    there = [(source, via) for source, _, via in detours]
    onward = [(via, target) for _, target, via in detours]
    relays = tuple(target for _, target, _ in detours)

    beyond = [lax.ppermute(coefficients, "bas", direct)]
    if detours:
        beyond.append(lax.ppermute(coefficients, "bas", [pair for pair in across if pair not in direct]))
    beside = lax.ppermute(coefficients, "bas", chip)
    tensor, coefficients = fetch(tensor, coefficients)
    cuts = (0, CUT, width)
    pattern = pattern.T
    few = most_needed(pattern, devices) <= FEW

    def exchange(held, count, pattern, coefficients, beside, beyond, tensor):
        (early, *late), whole = half_forms(held, count, cuts, relays, pattern, coefficients, beside, beyond, tensor)
        arrived = [[lax.ppermute(early, "bas", across)]] + [[lax.ppermute(part, "bas", direct)] for part in late]
        if detours:
            halfway = [lax.ppermute(part, "bas", there) for part in late]
            for got, part in zip(arrived[1:], halfway):
                got.append(lax.ppermute(part, "bas", onward))
        beside = [lax.ppermute(piece, "bas", chip) for piece in whole]
        half = blocks * slots // 2
        opened = gate(arrived[0][0])
        owned = [products(a, b, whole, whole, halfway[-1] if detours else opened) for a, b in zip(cuts, cuts[1:])]
        coded, earlier, summed = [], (opened,), ()
        for start, stop, own, got in zip(cuts, cuts[1:], owned, arrived):
            if start == 0:
                kept, sent = chunk_tiles(relays, 0, pattern, own, got, whole, beside, *earlier)
            else:
                near = products(start, stop, beside, whole, opened)
                kept, sent = chunk_tiles(relays, None, pattern, own, got, whole, [near], *earlier)
            mine = add_coded(half, kept, lax.ppermute(sent, "aux", flipped(layers, 1)), *summed)
            earlier = (mine,)
            mask = 2
            while mask < layers:
                mine = add_coded(half, mine, lax.ppermute(mine, "aux", flipped(layers, mask)))
                mask *= 2
            summed = (mine,)
            coded += [mine, lax.ppermute(mine, "aux", flipped(layers, 1))]
        return final_tiles((blocks, slots, width, width), coded)

    operands = (pattern, coefficients, beside, beyond, tensor)
    if blocks <= FEW:
        return exchange(blocks, 2, *operands)
    return lax.cond(few, functools.partial(exchange, FEW, 2), functools.partial(exchange, blocks, 2), *operands)


def solution(mesh):
    return jax.shard_map(
        body,
        mesh=mesh,
        in_specs=(P("bas", None), P("aux", "bas", None, None, None), P()),
        out_specs=P("bas", None, None, None),
        check_vma=False,
    )
```

```python
import functools
import itertools

import jax
import jax.numpy as jnp
import numpy as np
from jax import lax
from jax.experimental import pallas as pl
from jax.experimental.pallas import tpu as pltpu
from jax.sharding import PartitionSpec as P

CUT = 64
FEW = 3
SCALE_ROWS = 16
FULL = 32752.0
VMEM = pl.BlockSpec(memory_space=pltpu.VMEM)
ANY = pl.BlockSpec(memory_space=pl.ANY)
SMEM = pl.BlockSpec(memory_space=pltpu.SMEM)


def params(mib):
    return pltpu.CompilerParams(vmem_limit_bytes=mib << 20)


NO_COST = pl.CostEstimate(flops=0, bytes_accessed=0, transcendentals=0)
LONG = pl.CostEstimate(flops=6 * 10**9, bytes_accessed=0, transcendentals=0)


def piece_sizes(aux, count):
    return [aux // count + (k < aux % count) for k in range(count)]


def neighbour(device):
    return device + 2 * (device % 2) - 1


def most_needed(pattern, devices):
    rows = np.arange(pattern.shape[1])
    blocks = len(rows) // devices
    other = neighbour(np.arange(devices))
    wanted = other[:, None] * blocks + np.arange(blocks)
    wanted = np.where(((other >= 0) & (other < devices))[:, None], wanted, -2).astype(np.int32)
    own = rows // blocks == np.arange(devices)[:, None]
    listed = (pattern == wanted[:, :, None, None]) & own[:, None, None, :]
    return jnp.max(jnp.sum(jnp.any(listed, axis=(2, 3)), axis=1))


def needed(pattern, blocks, of, by):
    listed = [pattern[j, by * blocks + m] for j in range(pattern.shape[0]) for m in range(blocks)]
    return [functools.reduce(jnp.logical_or, [one == of * blocks + block for one in listed]) for block in range(blocks)]


def fetch_kernel(tensor, own, tensor_out, own_out, sems):
    copies = [
        pltpu.make_async_copy(own, own_out, sems.at[0]),
        pltpu.make_async_copy(tensor, tensor_out, sems.at[1]),
    ]
    for copy in copies:
        copy.start()
    for copy in copies:
        copy.wait()


def fetch(tensor, own):
    arrays = (tensor, own)
    return pl.pallas_call(
        fetch_kernel,
        out_shape=[jax.ShapeDtypeStruct(a.shape, a.dtype) for a in arrays],
        in_specs=[ANY] * 2,
        out_specs=[VMEM] * 2,
        scratch_shapes=[pltpu.SemaphoreType.DMA((2,))],
        compiler_params=params(8),
        cost_estimate=NO_COST,
    )(*(pltpu.with_memory_space_constraint(a, pltpu.HBM) for a in arrays))


def half_kernel(cuts, count, relays, pattern, own, *refs):
    outs = refs[-(len(cuts) - 1 + count) :]
    parts, pieces = outs[: len(cuts) - 1], outs[len(cuts) - 1 :]
    *across, beside, tensor = refs[: -len(outs)]
    aux, blocks, slots, width, _ = tensor.shape
    occupied = own.shape[1]
    sizes = piece_sizes(aux, count)
    owner = [(k, i) for k, size in enumerate(sizes) for i in range(size)]
    device = lax.axis_index("bas")
    relayed = functools.reduce(jnp.logical_or, [device == target for target in relays], False)
    held = parts[0].shape[0]
    other = neighbour(device)
    there = (other >= 0) & (other < lax.axis_size("bas"))
    if held < blocks:
        asked = needed(pattern, blocks, device, jnp.clip(other, 0, lax.axis_size("bas") - 1))
    packed = jnp.int32(0)
    for m in range(blocks):
        chosen = []
        for j in range(slots):
            place = pattern[j, device * blocks + m]
            group = place // blocks
            rows = pl.ds(pl.multiple_of(jnp.maximum(place, 0) % blocks * width, width), width)
            value = across[0][rows, :]
            if relays:
                value = jnp.where(relayed, across[1][rows, :], value)
            value = jnp.where(group == device ^ 1, beside[rows, :], value)
            value = jnp.where(group == device, own[rows, :], value)
            chosen.append(jnp.where(place < 0, jnp.zeros_like(value), value))
        chosen = jnp.concatenate(chosen, axis=0)
        for p in range(aux):
            row = jnp.concatenate([tensor[p, m, j] for j in range(slots)], axis=1)
            half = jnp.dot(row, chosen, preferred_element_type=jnp.float32).astype(jnp.bfloat16)
            piece, column = owner[p]
            pieces[piece][m, :, column * occupied : (column + 1) * occupied] = half
            for part, start, stop in zip(parts, cuts, cuts[1:]):
                if held == blocks:
                    part[m, :, p * occupied : (p + 1) * occupied] = half[start:stop]
                elif m < held:
                    part[packed, :, p * occupied : (p + 1) * occupied] = half[start:stop]
        if held <= m:

            @pl.when(packed < held)
            def _():
                for part, start, stop in zip(parts, cuts, cuts[1:]):
                    at = 0
                    for piece in pieces:
                        part[packed, :, at : at + piece.shape[2]] = piece[m, start:stop, :]
                        at += piece.shape[2]

        if held < blocks:
            packed += (asked[m] & there).astype(jnp.int32)


def half_forms(held, count, cuts, relays, pattern, own, beside, across, tensor):
    aux, blocks, slots, width, _ = tensor.shape
    depth = aux * own.shape[1]
    shapes = [(held, b - a, depth) for a, b in zip(cuts, cuts[1:])]
    shapes += [(blocks, width, size * own.shape[1]) for size in piece_sizes(aux, count)]
    outs = pl.pallas_call(
        functools.partial(half_kernel, cuts, count, relays),
        out_shape=[jax.ShapeDtypeStruct(shape, jnp.bfloat16) for shape in shapes],
        in_specs=[SMEM] + [VMEM] * (3 + len(across)),
        out_specs=[VMEM] * len(shapes),
        compiler_params=params(24),
        cost_estimate=NO_COST,
    )(pattern, own, *across, beside, tensor)
    return outs[:-count], outs[-count:]


def encode(tiles, coded, scales):
    rows = tiles[0].shape[0]
    scales[...] = jnp.zeros_like(scales)
    for t, tile in enumerate(tiles):
        most = jnp.max(jnp.abs(tile), axis=0, keepdims=True)
        power = jnp.ceil(jnp.log2(jnp.maximum(most, 2.0**-90)))
        scales[t : t + 1, :] = power
        whole = jnp.round(tile * (FULL * jnp.exp2(-power)))
        coded[t * rows : (t + 1) * rows, :] = whole.astype(jnp.int32).astype(jnp.int16)
    end = len(tiles) * rows
    coded[end : end + SCALE_ROWS, :] = scales[...].astype(jnp.int32).astype(jnp.int16)


def decode(coded, rows, count):
    end = count * rows
    scales = coded[end : end + SCALE_ROWS, :].astype(jnp.int32).astype(jnp.float32)
    scales = jnp.exp2(scales) * (1.0 / FULL)
    for t in range(count):
        value = coded[t * rows : (t + 1) * rows, :].astype(jnp.int32).astype(jnp.float32)
        yield value * scales[t : t + 1, :]


def times(rows, pieces):
    total = 0.0
    for k, piece in enumerate(pieces):
        left, right = rows(k), piece[...]
        total += lax.dot_general(
            left.reshape(-1, left.shape[2]),
            right.reshape(-1, right.shape[2]),
            (((1,), (1,)), ((), ())),
            preferred_element_type=jnp.float32,
        )
    return total


def product_kernel(count, start, stop, *refs):
    rows, whole, product = refs[:count], refs[count : 2 * count], refs[-1]
    product[...] = times(lambda k: rows[k][:, start:stop, :], whole)


def products(start, stop, rows, whole, *earlier):
    blocks, width, _ = whole[0].shape
    return pl.pallas_call(
        functools.partial(product_kernel, len(whole), start, stop),
        out_shape=jax.ShapeDtypeStruct((blocks * (stop - start), blocks * width), jnp.float32),
        in_specs=[VMEM] * (2 * len(whole)) + [ANY] * len(earlier),
        out_specs=VMEM,
        compiler_params=params(24),
        cost_estimate=NO_COST,
    )(*rows, *whole, *earlier)


def gate_kernel(_, out):
    out[...] = jnp.zeros_like(out)


def gate(earlier):
    return pl.pallas_call(
        gate_kernel,
        out_shape=jax.ShapeDtypeStruct((8, 128), jnp.float32),
        in_specs=[ANY],
        out_specs=VMEM,
        compiler_params=params(4),
        cost_estimate=LONG,
    )(earlier)


def tile_kernel(relays, count, pieces, start, pattern, own, *refs):
    across, whole, near = refs[:count], refs[count : count + pieces], refs[count + pieces : -7]
    kept, sent, far, close, scales, places, sem = refs[-7:]
    blocks, width, _ = whole[0].shape
    ends = list(itertools.accumulate([piece.shape[2] for piece in whole], initial=0))
    rows = across[0].shape[1]
    slots = pattern.shape[0]
    device, layer = lax.axis_index("bas"), lax.axis_index("aux")
    half = blocks * slots // 2
    copy = pltpu.make_async_copy(pattern, places, sem)
    copy.start()

    def multiply(source):
        far[...] = times(lambda k: source[:, :, ends[k] : ends[k + 1]], whole)

    if count > 1:
        relayed = functools.reduce(jnp.logical_or, [device == target for target in relays])
        pl.when(relayed)(lambda: multiply(across[1]))
        pl.when(jnp.logical_not(relayed))(lambda: multiply(across[0]))
    else:
        multiply(across[0])
    if start is None:
        close = near[0]
    else:
        close[...] = times(lambda k: near[k][:, start : start + rows, :], whole)
    copy.wait()
    held = far.shape[0] // rows
    if held < blocks:
        asked = needed(places, blocks, neighbour(device), device)

    def tile(t, parity):
        m = parity * (blocks // 2) + t // slots
        place = places[t % slots, device * blocks + m]
        group, block = place // blocks, jnp.maximum(place, 0) % blocks
        columns = pl.ds(pl.multiple_of(m * width, width), width)
        part = pl.ds(pl.multiple_of(block * rows, rows), rows), columns
        if held < blocks:
            before = [jnp.where(asked[i] & (i < block), 1, 0) for i in range(blocks)]
            block = jnp.minimum(sum(before), held - 1)
        value = far[pl.ds(pl.multiple_of(block * rows, rows), rows), columns]
        value = jnp.where(group == device ^ 1, close[part], value)
        value = jnp.where(group == device, own[part], value)
        return jnp.where(place < 0, 0.0, value)

    for t in range(half):
        kept[t * rows : (t + 1) * rows, :] = tile(t, layer % 2)
    encode([tile(t, 1 - layer % 2) for t in range(half)], sent, scales)


def chunk_tiles(relays, start, pattern, own, across, whole, near, *earlier):
    blocks, width, _ = whole[0].shape
    rows, slots = across[0].shape[1], pattern.shape[0]
    half = blocks * slots // 2
    product = (blocks * rows, blocks * width)
    held = across[0].shape[0]

    def kernel(*refs):
        given = 2 + len(across) + len(whole) + len(near)
        tile_kernel(relays, len(across), len(whole), start, *refs[:given], *refs[given + len(earlier) :])

    return pl.pallas_call(
        kernel,
        out_shape=[
            jax.ShapeDtypeStruct((half * rows, width), jnp.float32),
            jax.ShapeDtypeStruct((half * rows + SCALE_ROWS, width), jnp.int16),
        ],
        in_specs=[ANY] + [VMEM] * (1 + len(across) + len(whole) + len(near)) + [ANY] * len(earlier),
        out_specs=[VMEM] * 2,
        scratch_shapes=[
            pltpu.VMEM((held * rows, blocks * width), jnp.float32),
            pltpu.VMEM((8, 128) if start is None else product, jnp.float32),
            pltpu.VMEM((SCALE_ROWS, width), jnp.float32),
            pltpu.SMEM(pattern.shape, pattern.dtype),
            pltpu.SemaphoreType.DMA,
        ],
        compiler_params=params(24),
        cost_estimate=NO_COST,
    )(pattern, own, *across, *whole, *near, *earlier)


def add_kernel(count, mine, other, *rest):
    coded, scales = rest[-2:]
    rows = (coded.shape[0] - SCALE_ROWS) // count
    if mine.dtype == jnp.float32:
        held = [mine[t * rows : (t + 1) * rows, :] for t in range(count)]
    else:
        held = decode(mine, rows, count)
    encode([a + b for a, b in zip(held, decode(other, rows, count))], coded, scales)


def add_coded(count, mine, other, *earlier):
    return pl.pallas_call(
        functools.partial(add_kernel, count),
        out_shape=jax.ShapeDtypeStruct(other.shape, other.dtype),
        in_specs=[VMEM] * 2 + [ANY] * len(earlier),
        out_specs=VMEM,
        scratch_shapes=[pltpu.VMEM((SCALE_ROWS, other.shape[1]), jnp.float32)],
        compiler_params=params(8),
        cost_estimate=NO_COST,
    )(mine, other, *earlier)


def final_kernel(*refs):
    coded, out = refs[:-1], refs[-1]
    blocks, slots, width, _ = out.shape
    half = blocks * slots // 2
    layer = lax.axis_index("aux")
    for mine in range(2):
        base = jnp.where(layer % 2 == mine, 0, half)
        chunks = [list(decode(part, (part.shape[0] - SCALE_ROWS) // half, half)) for part in coded[mine::2]]
        for t in range(half):
            place = base + t
            out[place // slots, place % slots] = jnp.concatenate([chunk[t] for chunk in chunks], axis=0).T


def final_tiles(shape, coded):
    return pl.pallas_call(
        final_kernel,
        out_shape=jax.ShapeDtypeStruct(shape, jnp.float32),
        in_specs=[VMEM] * len(coded),
        out_specs=VMEM,
        compiler_params=params(8),
        cost_estimate=NO_COST,
    )(*coded)


def flipped(size, mask):
    return [(i, i ^ mask) for i in range(size)]


def body(coefficients, tensor, pattern):
    devices, layers = lax.axis_size("bas"), lax.axis_size("aux")
    _, blocks, slots, width, _ = tensor.shape
    chip = flipped(devices, 1)
    across = [pair for i in range(1, devices - 1, 2) for pair in ((i, i + 1), (i + 1, i))]
    detours = ((3, 4, 7), (4, 3, 0)) if devices == 8 else ()
    direct = [pair for pair in across if pair not in [d[:2] for d in detours]]
    there = [(source, via) for source, _, via in detours]
    onward = [(via, target) for _, target, via in detours]
    relays = tuple(target for _, target, _ in detours)

    beyond = [lax.ppermute(coefficients, "bas", direct)]
    if detours:
        beyond.append(lax.ppermute(coefficients, "bas", [pair for pair in across if pair not in direct]))
    beside = lax.ppermute(coefficients, "bas", chip)
    tensor, coefficients = fetch(tensor, coefficients)
    cuts = (0, CUT, width)
    pattern = pattern.T
    few = most_needed(pattern, devices) <= FEW

    def exchange(held, count, pattern, coefficients, beside, beyond, tensor):
        (early, *late), whole = half_forms(held, count, cuts, relays, pattern, coefficients, beside, beyond, tensor)
        arrived = [[lax.ppermute(early, "bas", across)]] + [[lax.ppermute(part, "bas", direct)] for part in late]
        if detours:
            halfway = [lax.ppermute(part, "bas", there) for part in late]
            for got, part in zip(arrived[1:], halfway):
                got.append(lax.ppermute(part, "bas", onward))
        beside = [lax.ppermute(piece, "bas", chip) for piece in whole]
        half = blocks * slots // 2
        opened = gate(arrived[0][0])
        owned = [products(a, b, whole, whole, halfway[-1] if detours else opened) for a, b in zip(cuts, cuts[1:])]
        coded, earlier, summed = [], (opened,), ()
        for start, stop, own, got in zip(cuts, cuts[1:], owned, arrived):
            if start == 0:
                kept, sent = chunk_tiles(relays, 0, pattern, own, got, whole, beside, *earlier)
            else:
                near = products(start, stop, beside, whole, opened)
                kept, sent = chunk_tiles(relays, None, pattern, own, got, whole, [near], *earlier)
            mine = add_coded(half, kept, lax.ppermute(sent, "aux", flipped(layers, 1)), *(summed if held == blocks else ()))
            earlier = (mine,)
            mask = 2
            while mask < layers:
                mine = add_coded(half, mine, lax.ppermute(mine, "aux", flipped(layers, mask)))
                mask *= 2
            summed = (mine,)
            coded += [mine, lax.ppermute(mine, "aux", flipped(layers, 1))]
        return final_tiles((blocks, slots, width, width), coded)

    operands = (pattern, coefficients, beside, beyond, tensor)
    if blocks <= FEW:
        return exchange(blocks, 2, *operands)
    return lax.cond(few, functools.partial(exchange, FEW, 2), functools.partial(exchange, blocks, 2), *operands)


def solution(mesh):
    return jax.shard_map(
        body,
        mesh=mesh,
        in_specs=(P("bas", None), P("aux", "bas", None, None, None), P()),
        out_specs=P("bas", None, None, None),
        check_vma=False,
    )
```

```python
import functools
import itertools

import jax
import jax.numpy as jnp
import numpy as np
from jax import lax
from jax.experimental import pallas as pl
from jax.experimental.pallas import tpu as pltpu
from jax.sharding import PartitionSpec as P

CUT = 64
FEW = 3
SCALE_ROWS = 16
FULL = 32752.0
VMEM = pl.BlockSpec(memory_space=pltpu.VMEM)
ANY = pl.BlockSpec(memory_space=pl.ANY)
SMEM = pl.BlockSpec(memory_space=pltpu.SMEM)


def params(mib):
    return pltpu.CompilerParams(vmem_limit_bytes=mib << 20)


NO_COST = pl.CostEstimate(flops=0, bytes_accessed=0, transcendentals=0)
LONG = pl.CostEstimate(flops=6 * 10**9, bytes_accessed=0, transcendentals=0)


def piece_sizes(aux, count):
    return [aux // count + (k < aux % count) for k in range(count)]


def neighbour(device):
    return device + 2 * (device % 2) - 1


def most_needed(pattern, devices):
    rows = np.arange(pattern.shape[1])
    blocks = len(rows) // devices
    other = neighbour(np.arange(devices))
    wanted = other[:, None] * blocks + np.arange(blocks)
    wanted = np.where(((other >= 0) & (other < devices))[:, None], wanted, -2).astype(np.int32)
    own = rows // blocks == np.arange(devices)[:, None]
    listed = (pattern == wanted[:, :, None, None]) & own[:, None, None, :]
    return jnp.max(jnp.sum(jnp.any(listed, axis=(2, 3)), axis=1))


def needed(pattern, blocks, of, by):
    listed = [pattern[j, by * blocks + m] for j in range(pattern.shape[0]) for m in range(blocks)]
    return [functools.reduce(jnp.logical_or, [one == of * blocks + block for one in listed]) for block in range(blocks)]


def fetch_kernel(tensor, own, tensor_out, own_out, sems):
    copies = [
        pltpu.make_async_copy(own, own_out, sems.at[0]),
        pltpu.make_async_copy(tensor, tensor_out, sems.at[1]),
    ]
    for copy in copies:
        copy.start()
    for copy in copies:
        copy.wait()


def fetch(tensor, own):
    arrays = (tensor, own)
    return pl.pallas_call(
        fetch_kernel,
        out_shape=[jax.ShapeDtypeStruct(a.shape, a.dtype) for a in arrays],
        in_specs=[ANY] * 2,
        out_specs=[VMEM] * 2,
        scratch_shapes=[pltpu.SemaphoreType.DMA((2,))],
        compiler_params=params(8),
        cost_estimate=NO_COST,
    )(*(pltpu.with_memory_space_constraint(a, pltpu.HBM) for a in arrays))


def half_kernel(cuts, count, relays, pattern, own, *refs):
    outs = refs[-(len(cuts) - 1 + count) :]
    parts, pieces = outs[: len(cuts) - 1], outs[len(cuts) - 1 :]
    *across, beside, tensor = refs[: -len(outs)]
    aux, blocks, slots, width, _ = tensor.shape
    occupied = own.shape[1]
    sizes = piece_sizes(aux, count)
    owner = [(k, i) for k, size in enumerate(sizes) for i in range(size)]
    device = lax.axis_index("bas")
    relayed = functools.reduce(jnp.logical_or, [device == target for target in relays], False)
    held = parts[0].shape[0]
    other = neighbour(device)
    there = (other >= 0) & (other < lax.axis_size("bas"))
    if held < blocks:
        asked = needed(pattern, blocks, device, jnp.clip(other, 0, lax.axis_size("bas") - 1))
    packed = jnp.int32(0)
    for m in range(blocks):
        chosen = []
        for j in range(slots):
            place = pattern[j, device * blocks + m]
            group = place // blocks
            rows = pl.ds(pl.multiple_of(jnp.maximum(place, 0) % blocks * width, width), width)
            value = across[0][rows, :]
            if relays:
                value = jnp.where(relayed, across[1][rows, :], value)
            value = jnp.where(group == device ^ 1, beside[rows, :], value)
            value = jnp.where(group == device, own[rows, :], value)
            chosen.append(jnp.where(place < 0, jnp.zeros_like(value), value))
        chosen = jnp.concatenate(chosen, axis=0)
        for p in range(aux):
            row = jnp.concatenate([tensor[p, m, j] for j in range(slots)], axis=1)
            half = jnp.dot(row, chosen, preferred_element_type=jnp.float32).astype(jnp.bfloat16)
            piece, column = owner[p]
            pieces[piece][m, :, column * occupied : (column + 1) * occupied] = half
            for part, start, stop in zip(parts, cuts, cuts[1:]):
                if held == blocks:
                    part[m, :, p * occupied : (p + 1) * occupied] = half[start:stop]
                elif m < held:
                    part[packed, :, p * occupied : (p + 1) * occupied] = half[start:stop]
        if held <= m:

            @pl.when(packed < held)
            def _():
                for part, start, stop in zip(parts, cuts, cuts[1:]):
                    at = 0
                    for piece in pieces:
                        part[packed, :, at : at + piece.shape[2]] = piece[m, start:stop, :]
                        at += piece.shape[2]

        if held < blocks:
            packed += (asked[m] & there).astype(jnp.int32)


def half_forms(held, count, cuts, relays, pattern, own, beside, across, tensor):
    aux, blocks, slots, width, _ = tensor.shape
    depth = aux * own.shape[1]
    shapes = [(held, b - a, depth) for a, b in zip(cuts, cuts[1:])]
    shapes += [(blocks, width, size * own.shape[1]) for size in piece_sizes(aux, count)]
    outs = pl.pallas_call(
        functools.partial(half_kernel, cuts, count, relays),
        out_shape=[jax.ShapeDtypeStruct(shape, jnp.bfloat16) for shape in shapes],
        in_specs=[SMEM] + [VMEM] * (3 + len(across)),
        out_specs=[VMEM] * len(shapes),
        compiler_params=params(24),
        cost_estimate=NO_COST,
    )(pattern, own, *across, beside, tensor)
    return outs[:-count], outs[-count:]


def encode(tiles, coded, scales):
    rows = tiles[0].shape[0]
    scales[...] = jnp.zeros_like(scales)
    for t, tile in enumerate(tiles):
        most = jnp.max(jnp.abs(tile), axis=0, keepdims=True)
        power = jnp.ceil(jnp.log2(jnp.maximum(most, 2.0**-90)))
        scales[t : t + 1, :] = power
        whole = jnp.round(tile * (FULL * jnp.exp2(-power)))
        coded[t * rows : (t + 1) * rows, :] = whole.astype(jnp.int32).astype(jnp.int16)
    end = len(tiles) * rows
    coded[end : end + SCALE_ROWS, :] = scales[...].astype(jnp.int32).astype(jnp.int16)


def decode(coded, rows, count):
    end = count * rows
    scales = coded[end : end + SCALE_ROWS, :].astype(jnp.int32).astype(jnp.float32)
    scales = jnp.exp2(scales) * (1.0 / FULL)
    for t in range(count):
        value = coded[t * rows : (t + 1) * rows, :].astype(jnp.int32).astype(jnp.float32)
        yield value * scales[t : t + 1, :]


def times(rows, pieces):
    total = 0.0
    for k, piece in enumerate(pieces):
        left, right = rows(k), piece[...]
        total += lax.dot_general(
            left.reshape(-1, left.shape[2]),
            right.reshape(-1, right.shape[2]),
            (((1,), (1,)), ((), ())),
            preferred_element_type=jnp.float32,
        )
    return total


def product_kernel(count, start, stop, *refs):
    rows, whole, product = refs[:count], refs[count : 2 * count], refs[-1]
    product[...] = times(lambda k: rows[k][:, start:stop, :], whole)


def products(start, stop, rows, whole, *earlier):
    blocks, width, _ = whole[0].shape
    return pl.pallas_call(
        functools.partial(product_kernel, len(whole), start, stop),
        out_shape=jax.ShapeDtypeStruct((blocks * (stop - start), blocks * width), jnp.float32),
        in_specs=[VMEM] * (2 * len(whole)) + [ANY] * len(earlier),
        out_specs=VMEM,
        compiler_params=params(24),
        cost_estimate=NO_COST,
    )(*rows, *whole, *earlier)


def gate_kernel(_, out):
    out[...] = jnp.zeros_like(out)


def gate(earlier):
    return pl.pallas_call(
        gate_kernel,
        out_shape=jax.ShapeDtypeStruct((8, 128), jnp.float32),
        in_specs=[ANY],
        out_specs=VMEM,
        compiler_params=params(4),
        cost_estimate=LONG,
    )(earlier)


def tile_kernel(relays, count, pieces, start, pattern, own, *refs):
    across, whole, near = refs[:count], refs[count : count + pieces], refs[count + pieces : -7]
    kept, sent, far, close, scales, places, sem = refs[-7:]
    blocks, width, _ = whole[0].shape
    ends = list(itertools.accumulate([piece.shape[2] for piece in whole], initial=0))
    rows = across[0].shape[1]
    slots = pattern.shape[0]
    device, layer = lax.axis_index("bas"), lax.axis_index("aux")
    half = blocks * slots // 2
    copy = pltpu.make_async_copy(pattern, places, sem)
    copy.start()

    def multiply(source):
        far[...] = times(lambda k: source[:, :, ends[k] : ends[k + 1]], whole)

    if count > 1:
        relayed = functools.reduce(jnp.logical_or, [device == target for target in relays])
        pl.when(relayed)(lambda: multiply(across[1]))
        pl.when(jnp.logical_not(relayed))(lambda: multiply(across[0]))
    else:
        multiply(across[0])
    if start is None:
        close = near[0]
    else:
        close[...] = times(lambda k: near[k][:, start : start + rows, :], whole)
    copy.wait()
    held = far.shape[0] // rows
    if held < blocks:
        asked = needed(places, blocks, neighbour(device), device)

    def tile(t, parity):
        m = parity * (blocks // 2) + t // slots
        place = places[t % slots, device * blocks + m]
        group, block = place // blocks, jnp.maximum(place, 0) % blocks
        columns = pl.ds(pl.multiple_of(m * width, width), width)
        part = pl.ds(pl.multiple_of(block * rows, rows), rows), columns
        if held < blocks:
            before = [jnp.where(asked[i] & (i < block), 1, 0) for i in range(blocks)]
            block = jnp.minimum(sum(before), held - 1)
        value = far[pl.ds(pl.multiple_of(block * rows, rows), rows), columns]
        value = jnp.where(group == device ^ 1, close[part], value)
        value = jnp.where(group == device, own[part], value)
        return jnp.where(place < 0, 0.0, value)

    for t in range(half):
        kept[t * rows : (t + 1) * rows, :] = tile(t, layer % 2)
    encode([tile(t, 1 - layer % 2) for t in range(half)], sent, scales)


def chunk_tiles(relays, start, pattern, own, across, whole, near, *earlier):
    blocks, width, _ = whole[0].shape
    rows, slots = across[0].shape[1], pattern.shape[0]
    half = blocks * slots // 2
    product = (blocks * rows, blocks * width)
    held = across[0].shape[0]

    def kernel(*refs):
        given = 2 + len(across) + len(whole) + len(near)
        tile_kernel(relays, len(across), len(whole), start, *refs[:given], *refs[given + len(earlier) :])

    return pl.pallas_call(
        kernel,
        out_shape=[
            jax.ShapeDtypeStruct((half * rows, width), jnp.float32),
            jax.ShapeDtypeStruct((half * rows + SCALE_ROWS, width), jnp.int16),
        ],
        in_specs=[ANY] + [VMEM] * (1 + len(across) + len(whole) + len(near)) + [ANY] * len(earlier),
        out_specs=[VMEM] * 2,
        scratch_shapes=[
            pltpu.VMEM((held * rows, blocks * width), jnp.float32),
            pltpu.VMEM((8, 128) if start is None else product, jnp.float32),
            pltpu.VMEM((SCALE_ROWS, width), jnp.float32),
            pltpu.SMEM(pattern.shape, pattern.dtype),
            pltpu.SemaphoreType.DMA,
        ],
        compiler_params=params(24),
        cost_estimate=NO_COST,
    )(pattern, own, *across, *whole, *near, *earlier)


def add_kernel(count, mine, other, *rest):
    coded, scales = rest[-2:]
    rows = (coded.shape[0] - SCALE_ROWS) // count
    if mine.dtype == jnp.float32:
        held = [mine[t * rows : (t + 1) * rows, :] for t in range(count)]
    else:
        held = decode(mine, rows, count)
    encode([a + b for a, b in zip(held, decode(other, rows, count))], coded, scales)


def add_coded(count, mine, other, *earlier):
    return pl.pallas_call(
        functools.partial(add_kernel, count),
        out_shape=jax.ShapeDtypeStruct(other.shape, other.dtype),
        in_specs=[VMEM] * 2 + [ANY] * len(earlier),
        out_specs=VMEM,
        scratch_shapes=[pltpu.VMEM((SCALE_ROWS, other.shape[1]), jnp.float32)],
        compiler_params=params(8),
        cost_estimate=NO_COST,
    )(mine, other, *earlier)


def final_kernel(*refs):
    coded, out = refs[:-1], refs[-1]
    blocks, slots, width, _ = out.shape
    half = blocks * slots // 2
    layer = lax.axis_index("aux")
    for mine in range(2):
        base = jnp.where(layer % 2 == mine, 0, half)
        chunks = [list(decode(part, (part.shape[0] - SCALE_ROWS) // half, half)) for part in coded[mine::2]]
        for t in range(half):
            place = base + t
            out[place // slots, place % slots] = jnp.concatenate([chunk[t] for chunk in chunks], axis=0).T


def final_tiles(shape, coded):
    return pl.pallas_call(
        final_kernel,
        out_shape=jax.ShapeDtypeStruct(shape, jnp.float32),
        in_specs=[VMEM] * len(coded),
        out_specs=VMEM,
        compiler_params=params(8),
        cost_estimate=NO_COST,
    )(*coded)


def flipped(size, mask):
    return [(i, i ^ mask) for i in range(size)]


def body(coefficients, tensor, pattern):
    devices, layers = lax.axis_size("bas"), lax.axis_size("aux")
    _, blocks, slots, width, _ = tensor.shape
    chip = flipped(devices, 1)
    across = [pair for i in range(1, devices - 1, 2) for pair in ((i, i + 1), (i + 1, i))]
    detours = ((3, 4, 7), (4, 3, 0)) if devices == 8 else ()
    direct = [pair for pair in across if pair not in [d[:2] for d in detours]]
    there = [(source, via) for source, _, via in detours]
    onward = [(via, target) for _, target, via in detours]
    relays = tuple(target for _, target, _ in detours)

    beyond = [lax.ppermute(coefficients, "bas", direct)]
    if detours:
        beyond.append(lax.ppermute(coefficients, "bas", [pair for pair in across if pair not in direct]))
    beside = lax.ppermute(coefficients, "bas", chip)
    tensor, coefficients = fetch(tensor, coefficients)
    cuts = (0, CUT, width)
    pattern = pattern.T
    few = most_needed(pattern, devices) <= FEW

    def exchange(held, count, pattern, coefficients, beside, beyond, tensor):
        (early, *late), whole = half_forms(held, count, cuts, relays, pattern, coefficients, beside, beyond, tensor)
        arrived = [[lax.ppermute(early, "bas", across)]] + [[lax.ppermute(part, "bas", direct)] for part in late]
        if detours:
            halfway = [lax.ppermute(part, "bas", there) for part in late]
            for got, part in zip(arrived[1:], halfway):
                got.append(lax.ppermute(part, "bas", onward))
        beside = [lax.ppermute(piece, "bas", chip) for piece in whole]
        half = blocks * slots // 2
        opened = gate(arrived[0][0])
        owned = [products(a, b, whole, whole, halfway[-1] if detours else opened) for a, b in zip(cuts, cuts[1:])]
        coded, earlier, summed = [], (opened,), ()
        for start, stop, own, got in zip(cuts, cuts[1:], owned, arrived):
            if start == 0:
                kept, sent = chunk_tiles(relays, 0, pattern, own, got, whole, beside, *earlier)
            else:
                near = products(start, stop, beside, whole, opened)
                kept, sent = chunk_tiles(relays, None, pattern, own, got, whole, [near], *earlier)
            mine = add_coded(half, kept, lax.ppermute(sent, "aux", flipped(layers, 1)), *(summed if held == blocks else ()))
            earlier = (mine,) if held == blocks else (sent,)
            mask = 2
            while mask < layers:
                mine = add_coded(half, mine, lax.ppermute(mine, "aux", flipped(layers, mask)))
                mask *= 2
            summed = (mine,)
            coded += [mine, lax.ppermute(mine, "aux", flipped(layers, 1))]
        return final_tiles((blocks, slots, width, width), coded)

    operands = (pattern, coefficients, beside, beyond, tensor)
    if blocks <= FEW:
        return exchange(blocks, 2, *operands)
    return lax.cond(few, functools.partial(exchange, FEW, 2), functools.partial(exchange, blocks, 2), *operands)


def solution(mesh):
    return jax.shard_map(
        body,
        mesh=mesh,
        in_specs=(P("bas", None), P("aux", "bas", None, None, None), P()),
        out_specs=P("bas", None, None, None),
        check_vma=False,
    )
```
